512 devices in a mesh: det: 32 (over y, x, core), shot: 16 (over z).
Axes of the slice: x: 4, y: 4, z: 16, core: 2. Of those that a mesh axis runs over, the one named last changes fastest.
Arguments:
- features: float32 [32768, 16384], P('det', 'shot'), may hold values from -200 to 200
- pairs: int32 [512, 2], P('det'), may hold values from 0 to 127, as said below
Outputs:
- tiles: float32 [256, 512, 256], P('shot', 'det')
The draws below stay inside these ranges and needn't reach their ends.
Inputs may be any that keep to these rules, and one draw needn't show every extreme that they name: Row p of pairs belongs to owner o = p // 16: its first block lies in o * 4 to o * 4 + 3, and its second block differs from the first by at most 2; the pairs of one owner are distinct. Every owner but the last has the pair (o * 4 + 3, o * 4 + 5), and every owner but the first has the pair (o * 4, o * 4 - 2).
All inputs are finite; a program needn't handle non-finite values.
Results may differ from the reference program's by a relative error of at most 0.0003.
Values sent between devices are 32-bit elements; how exact they have to be, the bound alone decides.
No kernel may reach another device: no remote copies, remote signals or barrier semaphores. Data moves between devices by JAX's collectives and lax.ppermute only.
A program may use at most 128 MiB of HBM per device.

```python
import jax
import jax.numpy as jnp
from jax import lax

BLK = 256
B_DEV = 4
PAIR_DEV = 16
REACH = 2
NBLK = 128
NDET = 32768
SHOTS = 16384
N_DET = 32


def draw_features(key, part):
    key = jax.random.fold_in(key, 11)
    keys = jax.random.split(key, 3)
    ramp = jnp.exp(jnp.log(3.0) * jnp.arange(SHOTS, dtype=jnp.float32) / SHOTS)
    offset = jax.random.uniform(keys[1], (NDET, 1), jnp.float32, -2.0, 2.0)
    noise = jnp.clip(jax.random.normal(keys[0], (NDET, SHOTS), jnp.float32), -5.0, 5.0)
    scales = jnp.exp(jax.random.uniform(keys[2], (NDET, 1), jnp.float32, 0.0, jnp.log(10.0)))
    mixed = noise + 0.3 * jnp.roll(noise, 1, axis=0)
    return (offset + scales * mixed * ramp[None, :]).astype(jnp.float32)


def draw_pairs(key, part):
    key = jax.random.fold_in(key, 23)
    spread = 2 * REACH + 1
    count = B_DEV * spread
    owners = jnp.arange(N_DET, dtype=jnp.int32)
    combo = jnp.arange(count, dtype=jnp.int32)
    local = combo // spread
    step = combo % spread - REACH
    first = owners[:, None] * B_DEV + local[None, :]
    second = first + step[None, :]
    valid = (second >= 0) & (second <= NBLK - 1)
    scores = jax.random.randint(key, (N_DET, count), 0, 1 << 16) * count + combo[None, :]
    upper_edge = (local == B_DEV - 1) & (step == REACH)
    lower_edge = (local == 0) & (step == -REACH)
    scores = jnp.where(upper_edge[None, :], -2, scores)
    scores = jnp.where(lower_edge[None, :], -1, scores)
    scores = jnp.where(valid, scores, scores + (1 << 28))
    order = jnp.argsort(scores, axis=1, stable=True)[:, :PAIR_DEV]
    chosen_first = jnp.take_along_axis(first, order, axis=1).reshape(-1)
    chosen_second = jnp.take_along_axis(second, order, axis=1).reshape(-1)
    return jnp.stack([chosen_first, chosen_second], axis=1).astype(jnp.int32)


def setup_inputs(seed: int = 0) -> dict:
    streams_of = jax.random.split(jax.random.key(seed), 3)
    return {
        "features": draw_features(jax.random.fold_in(streams_of[2], 71), 0),
        "pairs": draw_pairs(jax.random.fold_in(streams_of[2], 71), 0),
    }


def reference(features, pairs):
    sums = lax.optimization_barrier(jnp.sum(features, axis=1))
    squares = lax.optimization_barrier(jnp.sum(features * features, axis=1))
    mean = sums / SHOTS
    inverse = lax.rsqrt(squares / SHOTS - mean * mean + 1e-06)
    standard = (features - mean[:, None]) * inverse[:, None]
    scale = 1.0 / jnp.sqrt(jnp.float32(SHOTS))

    def one_tile(pair):
        first = lax.dynamic_slice_in_dim(standard, (pair[0] * BLK).astype(jnp.int32), BLK, 0)
        second = lax.dynamic_slice_in_dim(standard, (pair[1] * BLK).astype(jnp.int32), BLK, 0)
        return jnp.dot(first, second.T, precision=lax.Precision.HIGHEST, preferred_element_type=jnp.float32) * scale
    stacked = lax.map(one_tile, pairs)
    return jnp.transpose(stacked, (1, 0, 2))
```

```python
import functools

import jax
import jax.numpy as jnp
from jax import lax
from jax.experimental import pallas as pl
from jax.experimental.pallas import tpu as pltpu
from jax.sharding import PartitionSpec as P

BLK = 256
OWN = 4
EARLY = 10
MAIN = 14
PAIRS = 16
SHARDS = 16
ROWS = BLK // SHARDS
REST = PAIRS - MAIN
CHUNKS = 4 * REST * ROWS
PART = REST * ROWS
F32 = jnp.float32
BF16 = jnp.bfloat16
SMEM = pltpu.SMEM


def split_block(x, hi_ref, lo_ref, at, stats_ref, row):
    count = x.shape[1]
    mean = jnp.sum(x, axis=1, keepdims=True) * (1.0 / count)
    centered = x - mean
    squares = jnp.sum(centered * centered, axis=1, keepdims=True)
    hi = centered.astype(BF16)
    hi_ref[pl.ds(at, BLK), :] = hi
    lo_ref[pl.ds(at, BLK), :] = (centered - hi.astype(F32)).astype(BF16)
    lane = lax.broadcasted_iota(jnp.int32, (BLK, 128), 1)
    both = jnp.where(lane < 8, jnp.broadcast_to(mean, (BLK, 128)), jnp.broadcast_to(squares, (BLK, 128)))
    flat = jnp.transpose(both)
    stats_ref[0, pl.ds(row, 1), :] = flat[0:1, :]
    stats_ref[1, pl.ds(row, 1), :] = flat[8:9, :]


def product(hi_a, lo_a, hi_b, lo_b):
    dims = (((1,), (1,)), ((), ()))
    dot = functools.partial(lax.dot_general, dimension_numbers=dims, preferred_element_type=F32)
    return dot(hi_a, hi_b) + (dot(hi_a, lo_b) + dot(lo_a, hi_b))


def early_kernel(
    pairs_ref, base_ref, x_ref,
    tiles_ref, hi_ref, lo_ref, stats_ref, lower_ref, upper_ref, first_ref, second_ref, slot_ref,
):
    step = pl.program_id(0)

    @pl.when(step == 0)
    def _():
        base = base_ref[0]

        def kind_of(p):
            second = pairs_ref[p, 1] - base
            inside = jnp.logical_and(second >= 0, second < OWN)
            near = jnp.logical_and(second >= -1, second <= OWN)
            return jnp.where(inside, 0, jnp.where(near, 1, 2))

        kinds = [kind_of(p) for p in range(PAIRS)]
        n_in = sum((k == 0).astype(jnp.int32) for k in kinds)
        n_near = sum((k == 1).astype(jnp.int32) for k in kinds)
        counts = [jnp.int32(0), n_in, n_in + n_near]
        for p in range(PAIRS):
            k = kinds[p]
            slot = jnp.where(k == 0, counts[0], jnp.where(k == 1, counts[1], counts[2]))
            counts = [c + (k == i).astype(jnp.int32) for i, c in enumerate(counts)]
            slot_ref[p] = slot
            first_ref[slot] = pairs_ref[p, 0] - base
            second_ref[slot] = pairs_ref[p, 1] - base

    @pl.when(step < OWN)
    def _():
        split_block(x_ref[...], hi_ref, lo_ref, pl.multiple_of(step * BLK, BLK), stats_ref, step)

    @pl.when(step == 1)
    def _():
        lower_ref[...] = x_ref[...]

    @pl.when(step == 2)
    def _():
        upper_ref[...] = x_ref[...]

    @pl.when(step >= OWN)
    def _():
        slot = step - OWN
        a = pl.ds(pl.multiple_of(first_ref[slot] * BLK, BLK), BLK)
        b = pl.ds(pl.multiple_of(second_ref[slot] * BLK, BLK), BLK)
        tile = product(hi_ref[a, :], lo_ref[a, :], hi_ref[b, :], lo_ref[b, :])
        tiles_ref[...] = tile.reshape(SHARDS, 1, ROWS, BLK)


def early(pairs, base, features):
    rows, shots = features.shape
    return pl.pallas_call(
        early_kernel,
        grid=(OWN + EARLY,),
        in_specs=[
            pl.BlockSpec(memory_space=SMEM),
            pl.BlockSpec(memory_space=SMEM),
            pl.BlockSpec((BLK, shots), lambda i: (jnp.minimum(i, OWN - 1), 0)),
        ],
        out_specs=[
            pl.BlockSpec((SHARDS, 1, ROWS, BLK), lambda i: (0, jnp.maximum(i - OWN, 0), 0, 0)),
            pl.BlockSpec((rows, shots), lambda i: (0, 0)),
            pl.BlockSpec((rows, shots), lambda i: (0, 0)),
            pl.BlockSpec((2, OWN, BLK), lambda i: (0, 0, 0)),
            pl.BlockSpec((BLK, shots), lambda i: (0, 0)),
            pl.BlockSpec((BLK, shots), lambda i: (0, 0)),
            pl.BlockSpec(memory_space=SMEM),
            pl.BlockSpec(memory_space=SMEM),
            pl.BlockSpec(memory_space=SMEM),
        ],
        out_shape=[
            pltpu.HBM((SHARDS, MAIN, ROWS, BLK), F32),
            jax.ShapeDtypeStruct((rows, shots), BF16),
            jax.ShapeDtypeStruct((rows, shots), BF16),
            jax.ShapeDtypeStruct((2, OWN, BLK), F32),
            jax.ShapeDtypeStruct((BLK, shots), F32),
            jax.ShapeDtypeStruct((BLK, shots), F32),
            jax.ShapeDtypeStruct((PAIRS,), jnp.int32),
            jax.ShapeDtypeStruct((PAIRS,), jnp.int32),
            jax.ShapeDtypeStruct((PAIRS,), jnp.int32),
        ],
        compiler_params=pltpu.CompilerParams(vmem_limit_bytes=40 << 20),
        cost_estimate=pl.CostEstimate(flops=6 * EARLY * BLK * BLK * shots, bytes_accessed=12 << 20, transcendentals=0),
        name="early_tiles",
    )(pairs, base, features)


def near_kernel(
    first_ref, second_ref, hi_a, lo_a, hi_b, lo_b, below_ref, above_ref, _, tiles_ref, hhi, hlo, unused
):
    step = pl.program_id(0)

    @pl.when(step == 0)
    def _():
        split_block(below_ref[...], hhi, hlo, 0, unused, 0)
        split_block(above_ref[...], hhi, hlo, BLK, unused, 1)

    second = second_ref[EARLY + step]
    inside = jnp.logical_and(second >= 0, second < OWN)

    @pl.when(inside)
    def _():
        tile = product(hi_a[...], lo_a[...], hi_b[...], lo_b[...])
        tiles_ref[...] = tile.reshape(SHARDS, 1, ROWS, BLK)

    @pl.when(jnp.logical_not(inside))
    def _():
        b = pl.ds(pl.multiple_of(jnp.where(second < 0, 0, BLK), BLK), BLK)
        tile = product(hi_a[...], lo_a[...], hhi[b, :], hlo[b, :])
        tiles_ref[...] = tile.reshape(SHARDS, 1, ROWS, BLK)


def near(first, second, hi, lo, below, above, tiles):
    shots = hi.shape[1]
    left = pl.BlockSpec((BLK, shots), lambda i, a, b: (a[EARLY + i], 0))
    right = pl.BlockSpec((BLK, shots), lambda i, a, b: (jnp.clip(b[EARLY + i], 0, OWN - 1), 0))
    halo = pl.BlockSpec((BLK, shots), lambda i, a, b: (0, 0))
    return pl.pallas_call(
        near_kernel,
        grid_spec=pltpu.PrefetchScalarGridSpec(
            num_scalar_prefetch=2,
            grid=(MAIN - EARLY,),
            in_specs=[left, left, right, right, halo, halo, pl.BlockSpec(memory_space=pl.ANY)],
            out_specs=pl.BlockSpec((SHARDS, 1, ROWS, BLK), lambda i, a, b: (0, EARLY + i, 0, 0)),
            scratch_shapes=[
                pltpu.VMEM((2 * BLK, shots), BF16),
                pltpu.VMEM((2 * BLK, shots), BF16),
                pltpu.VMEM((2, 8, BLK), F32),
            ],
        ),
        out_shape=pltpu.HBM(tiles.shape, F32),
        input_output_aliases={8: 0},
        compiler_params=pltpu.CompilerParams(vmem_limit_bytes=40 << 20),
        cost_estimate=pl.CostEstimate(flops=1 << 20, bytes_accessed=1 << 20, transcendentals=0),
        name="near_tiles",
    )(first, second, hi, lo, hi, lo, below, above, tiles)


def far_kernel(
    first_ref, second_ref, me_ref, hi_ref, lo_ref, far_below, below, above, far_above, own_ref,
    keep_ref, one_ref, two_ref, three_ref, stats_ref, hhi, hlo, full,
):
    outs = (keep_ref, one_ref, two_ref, three_ref)
    for place, ref in enumerate((far_below, below, above, far_above)):
        split_block(ref[...], hhi, hlo, place * BLK, stats_ref, place)
    me = me_ref[0]
    for t in range(REST):
        second = second_ref[MAIN + t]
        a = pl.ds(pl.multiple_of(first_ref[MAIN + t] * BLK, BLK), BLK)
        inside = jnp.logical_and(second >= 0, second < OWN)

        @pl.when(inside)
        def _():
            b = pl.ds(pl.multiple_of(jnp.clip(second, 0, OWN - 1) * BLK, BLK), BLK)
            full[...] = product(hi_ref[a, :], lo_ref[a, :], hi_ref[b, :], lo_ref[b, :])

        @pl.when(jnp.logical_not(inside))
        def _():
            place = jnp.where(second < 0, second + 2, second - 2)
            b = pl.ds(pl.multiple_of(jnp.clip(place, 0, 3) * BLK, BLK), BLK)
            full[...] = product(hi_ref[a, :], lo_ref[a, :], hhi[b, :], hlo[b, :])

        for ahead in range(SHARDS):
            shard = lax.rem(me - ahead + SHARDS, SHARDS)
            part = full[pl.ds(pl.multiple_of(shard * ROWS, ROWS), ROWS), :]
            at = (ahead // 4 * REST + t) * ROWS
            outs[ahead % 4][at : at + ROWS, :] = part
    for out in outs:
        for kind in range(2):
            at = CHUNKS + 8 * kind
            out[at : at + 2, :] = stats_ref[kind, 0:2, :]
            out[at + 2 : at + 6, :] = own_ref[kind]
            out[at + 6 : at + 8, :] = stats_ref[kind, 2:4, :]


def far(first, second, me, hi, lo, far_below, below, above, far_above, own):
    shots = hi.shape[1]
    vmem = pl.BlockSpec(memory_space=pltpu.VMEM)
    smem = pl.BlockSpec(memory_space=SMEM)
    return pl.pallas_call(
        far_kernel,
        in_specs=[smem] * 3 + [vmem] * 7,
        out_specs=[vmem] * 4,
        out_shape=[jax.ShapeDtypeStruct((CHUNKS + 16, BLK), F32)] * 4,
        scratch_shapes=[
            pltpu.VMEM((2, 4, BLK), F32),
            pltpu.VMEM((4 * BLK, shots), BF16),
            pltpu.VMEM((4 * BLK, shots), BF16),
            pltpu.VMEM((BLK, BLK), F32),
        ],
        compiler_params=pltpu.CompilerParams(vmem_limit_bytes=40 << 20),
        cost_estimate=pl.CostEstimate(flops=6 * 2 * BLK * BLK * shots, bytes_accessed=9 << 20, transcendentals=0),
        name="far_tiles",
    )(first, second, me, hi, lo, far_below, below, above, far_above, own)


def merge_kernel(keep_ref, one_ref, two_ref, three_ref, *outs):
    ins = (keep_ref, one_ref, two_ref, three_ref)
    for k, out in enumerate(outs):
        here, before = pl.ds(k * PART, PART), pl.ds((k + 3) % 4 * PART, PART)
        out[:PART, :] = (keep_ref[here, :] + one_ref[here, :]) + (two_ref[here, :] + three_ref[before, :])
        for i, ref in enumerate(ins):
            out[PART + 8 * i : PART + 8 * i + 8, :] = ref[CHUNKS : CHUNKS + 8, :]
        out[PART + 32 :, :] = sum(ref[CHUNKS + 8 :, :] for ref in ins)


def merge(*packs):
    vmem = pl.BlockSpec(memory_space=pltpu.VMEM)
    return pl.pallas_call(
        merge_kernel,
        in_specs=[vmem] * 4,
        out_specs=[vmem] * 4,
        out_shape=[jax.ShapeDtypeStruct((PART + 40, BLK), F32)] * 4,
        cost_estimate=pl.CostEstimate(flops=1 << 17, bytes_accessed=1 << 20, transcendentals=0),
        name="merge",
    )(*packs)


def factors_kernel(
    count, first_ref, second_ref, me_ref, one_ref, two_ref, three_ref, four_ref, shift_ref, scale_ref, turned, dev, inv
):
    packs = (one_ref, two_ref, three_ref, four_ref)
    shards = SHARDS
    total = shards * count
    means = jnp.concatenate([ref[PART : PART + 32, :].reshape(4, 8, BLK) for ref in packs], axis=0)
    mean = jnp.sum(means, axis=0) * (1.0 / shards)
    away = means - mean[None]
    squares = sum(ref[PART + 32 :, :] for ref in packs) + count * jnp.sum(away * away, axis=0)
    inverse = lax.rsqrt(squares * (1.0 / total) + 1e-06)
    inv[...] = inverse
    for block in range(8):
        dev[block] = away[:, block, :]
    for block in range(OWN):
        column = jnp.concatenate(
            [away[:, 2 + block, :], jnp.broadcast_to(inverse[2 + block : 3 + block, :], (128 - shards, BLK))], axis=0
        )
        turned[block] = jnp.transpose(column)
    mine = pl.ds(pl.multiple_of(me_ref[0] * ROWS, ROWS), ROWS)
    for slot in range(PAIRS):
        a = first_ref[slot]
        b = second_ref[slot] + 2
        left = turned[a, mine, :]
        shift_ref[slot] = count * jnp.dot(
            left[:, :shards], dev[b], precision=lax.Precision.HIGHEST, preferred_element_type=F32
        )
        scale_ref[slot] = left[:, shards : shards + 1] * inv[pl.ds(b, 1), :] * (1.0 / total**0.5)


def factors(count, first, second, me, *packs):
    vmem = pl.BlockSpec(memory_space=pltpu.VMEM)
    smem = pl.BlockSpec(memory_space=SMEM)
    return pl.pallas_call(
        functools.partial(factors_kernel, count),
        in_specs=[smem] * 3 + [vmem] * 4,
        out_specs=[vmem] * 2,
        out_shape=[jax.ShapeDtypeStruct((PAIRS, ROWS, BLK), F32)] * 2,
        scratch_shapes=[
            pltpu.VMEM((OWN, BLK, 128), F32),
            pltpu.VMEM((8, SHARDS, BLK), F32),
            pltpu.VMEM((8, BLK), F32),
        ],
        cost_estimate=pl.CostEstimate(flops=1 << 26, bytes_accessed=2 << 20, transcendentals=2048),
        name="factors",
    )(first, second, me, *packs)


def finish_kernel(slot_ref, main_ref, own_ref, one_ref, two_ref, three_ref, shift_ref, scale_ref, out_ref, all_ref):
    all_ref[:MAIN] = (main_ref[...] + shift_ref[:MAIN]) * scale_ref[:MAIN]
    rest = (own_ref[:PART, :] + one_ref[:PART, :]) + (two_ref[:PART, :] + three_ref[:PART, :])
    rest = rest.reshape(REST, ROWS, BLK)
    all_ref[MAIN:] = (rest + shift_ref[MAIN:]) * scale_ref[MAIN:]
    for p in range(PAIRS):
        out_ref[:, p, :] = all_ref[slot_ref[p]]


def finish(slot, main, own, one, two, three, shift, scale):
    vmem = pl.BlockSpec(memory_space=pltpu.VMEM)
    return pl.pallas_call(
        finish_kernel,
        in_specs=[pl.BlockSpec(memory_space=SMEM)] + [vmem] * 7,
        out_specs=vmem,
        out_shape=jax.ShapeDtypeStruct((ROWS, PAIRS, BLK), F32),
        scratch_shapes=[pltpu.VMEM((PAIRS, ROWS, BLK), F32)],
        cost_estimate=pl.CostEstimate(flops=1 << 18, bytes_accessed=1 << 20, transcendentals=0),
        name="finish",
    )(slot, main, own, one, two, three, shift, scale)


def on_device(features, pairs):
    shots = features.shape[1]
    owners, shards = lax.axis_size("det"), lax.axis_size("shot")
    base = (lax.axis_index("det") * OWN).astype(jnp.int32).reshape(1)
    me = lax.axis_index("shot").astype(jnp.int32).reshape(1)
    up = [(i, i + 1) for i in range(owners - 1)]
    down = [(i + 1, i) for i in range(owners - 1)]

    def block(x, k):
        return lax.slice_in_dim(x, k * BLK, (k + 1) * BLK, axis=0)

    def shifted(x, by):
        return lax.ppermute(x, "shot", [(i, (i + by) % shards) for i in range(shards)])

    features, top, bottom = lax.optimization_barrier((features, block(features, 3), block(features, 0)))
    below = lax.ppermute(top, "det", up)
    above = lax.ppermute(bottom, "det", down)
    tiles, hi, lo, own_stats, lower, upper, first, second, slot = early(
        pairs, base, pltpu.with_memory_space_constraint(features, pltpu.HBM)
    )
    far_below = lax.ppermute(upper, "det", up)
    far_above = lax.ppermute(lower, "det", down)
    tiles = near(first, second, hi, lo, below, above, tiles)
    main = lax.psum_scatter(
        tiles.reshape(SHARDS * MAIN * ROWS, BLK), "shot", scatter_dimension=0, tiled=True
    ).reshape(MAIN, ROWS, BLK)

    hi, tiles = lax.optimization_barrier((hi, tiles))
    keep, one, two, three = far(first, second, me, hi, lo, far_below, below, above, far_above, own_stats)
    own, one, two, three = merge(keep, shifted(one, -1), shifted(two, -2), shifted(three, 1))
    packs = own, shifted(one, -4), shifted(two, -8), shifted(three, 4)
    shift, scale = factors(float(shots), first, second, me, *packs)
    return finish(slot, main, *packs, shift, scale)


def solution(mesh):
    in_specs = (P("det", "shot"), P("det", None))
    out_specs = P("shot", "det", None)
    return jax.shard_map(on_device, mesh=mesh, in_specs=in_specs, out_specs=out_specs, check_vma=False)
```

```python
import functools

import jax
import jax.numpy as jnp
from jax import lax
from jax.experimental import pallas as pl
from jax.experimental.pallas import tpu as pltpu
from jax.sharding import PartitionSpec as P

BLK = 256
OWN = 4
EARLY = 10
MADE = 16
PAIRS = 16
HOME_A, HOME_B = 16, 17
SLOTS = 18
SHARDS = 16
ROWS = BLK // SHARDS
F32 = jnp.float32
BF16 = jnp.bfloat16
SMEM = pltpu.SMEM


def split_block(x, hi_ref, lo_ref, at, stats_ref, row):
    count = x.shape[1]
    mean = jnp.sum(x, axis=1, keepdims=True) * (1.0 / count)
    centered = x - mean
    squares = jnp.sum(centered * centered, axis=1, keepdims=True)
    hi = centered.astype(BF16)
    hi_ref[pl.ds(at, BLK), :] = hi
    lo_ref[pl.ds(at, BLK), :] = (centered - hi.astype(F32)).astype(BF16)
    lane = lax.broadcasted_iota(jnp.int32, (BLK, 128), 1)
    both = jnp.where(lane < 8, jnp.broadcast_to(mean, (BLK, 128)), jnp.broadcast_to(squares, (BLK, 128)))
    flat = jnp.transpose(both)
    stats_ref[0, pl.ds(row, 1), :] = flat[0:1, :]
    stats_ref[1, pl.ds(row, 1), :] = flat[8:9, :]


def product(hi_a, lo_a, hi_b, lo_b):
    dims = (((1,), (1,)), ((), ()))
    dot = functools.partial(lax.dot_general, dimension_numbers=dims, preferred_element_type=F32)
    return dot(hi_a, hi_b) + (dot(hi_a, lo_b) + dot(lo_a, hi_b))


def borders_kernel(core_ref, x_ref, a_ref, b_ref, sems):
    core = core_ref[0]
    to_a = pltpu.make_async_copy(x_ref.at[pl.ds(core * 3 * BLK, BLK), :], a_ref, sems.at[0])
    to_b = pltpu.make_async_copy(x_ref.at[pl.ds((1 - core) * 3 * BLK, BLK), :], b_ref, sems.at[1])
    to_a.start()
    to_b.start()
    to_a.wait()
    to_b.wait()


def borders(core, features):
    shots = features.shape[1]
    return pl.pallas_call(
        borders_kernel,
        in_specs=[pl.BlockSpec(memory_space=SMEM), pl.BlockSpec(memory_space=pl.ANY)],
        out_specs=[pl.BlockSpec(memory_space=pl.ANY)] * 2,
        out_shape=[jax.ShapeDtypeStruct((BLK, shots), F32)] * 2,
        scratch_shapes=[pltpu.SemaphoreType.DMA((2,))],
        cost_estimate=pl.CostEstimate(flops=0, bytes_accessed=4 << 20, transcendentals=0),
        name="borders",
    )(core, pltpu.with_memory_space_constraint(features, pltpu.HBM))


def assign(pairs_ref, base, core, first_ref, second_ref, slot_ref):
    def kind_of(p):
        second = pairs_ref[p, 1] - base
        inside = jnp.logical_and(second >= 0, second < OWN)
        near = jnp.logical_and(second >= -1, second <= OWN)
        with_a = (second < 0) == (core == 0)
        return jnp.where(inside, 0, jnp.where(near, jnp.where(with_a, 2, 1), jnp.where(with_a, 3, 4)))

    for slot in range(MADE, SLOTS):
        first_ref[slot] = 0
        second_ref[slot] = 0
    first_ref[14] = jnp.where(core == 0, OWN, -1)
    second_ref[14] = jnp.where(core == 0, 2, 1)
    first_ref[15] = jnp.where(core == 0, -1, OWN)
    second_ref[15] = jnp.where(core == 0, 1, 2)
    kinds = [kind_of(p) for p in range(PAIRS)]
    places = [jnp.int32(0)]
    for k in range(2):
        places.append(places[-1] + sum((kind == k).astype(jnp.int32) for kind in kinds))
    for p, kind in enumerate(kinds):
        place = jnp.where(kind == 0, places[0], jnp.where(kind == 1, places[1], places[2]))
        place = jnp.where(place >= 14, 15, place)
        slot = jnp.where(kind == 3, HOME_A, jnp.where(kind == 4, HOME_B, place))
        places = [place + (kind == k).astype(jnp.int32) for k, place in enumerate(places)]
        slot_ref[p] = slot
        first_ref[slot] = pairs_ref[p, 0] - base
        second_ref[slot] = pairs_ref[p, 1] - base


def early_kernel(
    pairs_ref, place_ref, x_ref, tiles_ref, hi_ref, lo_ref, stats_ref, first_ref, second_ref, slot_ref
):
    step = pl.program_id(0)

    @pl.when(step == 0)
    def _():
        assign(pairs_ref, place_ref[0], place_ref[1], first_ref, second_ref, slot_ref)

    @pl.when(step < OWN)
    def _():
        split_block(x_ref[...], hi_ref, lo_ref, pl.multiple_of(step * BLK, BLK), stats_ref, step)

    @pl.when(step >= OWN)
    def _():
        slot = step - OWN
        a = pl.ds(pl.multiple_of(first_ref[slot] * BLK, BLK), BLK)
        b = pl.ds(pl.multiple_of(second_ref[slot] * BLK, BLK), BLK)
        tile = product(hi_ref[a, :], lo_ref[a, :], hi_ref[b, :], lo_ref[b, :])
        tiles_ref[...] = tile.reshape(SHARDS, 1, ROWS, BLK)


def early(pairs, place, features):
    rows, shots = features.shape
    smem = pl.BlockSpec(memory_space=SMEM)
    return pl.pallas_call(
        early_kernel,
        grid=(OWN + EARLY,),
        in_specs=[smem, smem, pl.BlockSpec((BLK, shots), lambda i: (jnp.minimum(i, OWN - 1), 0))],
        out_specs=[
            pl.BlockSpec((SHARDS, 1, ROWS, BLK), lambda i: (0, jnp.maximum(i - OWN, 0), 0, 0)),
            pl.BlockSpec((rows, shots), lambda i: (0, 0)),
            pl.BlockSpec((rows, shots), lambda i: (0, 0)),
            pl.BlockSpec((2, OWN, BLK), lambda i: (0, 0, 0)),
            smem,
            smem,
            smem,
        ],
        out_shape=[
            pltpu.HBM((SHARDS, MADE, ROWS, BLK), F32),
            jax.ShapeDtypeStruct((rows, shots), BF16),
            jax.ShapeDtypeStruct((rows, shots), BF16),
            jax.ShapeDtypeStruct((2, OWN, BLK), F32),
            jax.ShapeDtypeStruct((SLOTS,), jnp.int32),
            jax.ShapeDtypeStruct((SLOTS,), jnp.int32),
            jax.ShapeDtypeStruct((PAIRS,), jnp.int32),
        ],
        compiler_params=pltpu.CompilerParams(vmem_limit_bytes=40 << 20),
        cost_estimate=pl.CostEstimate(flops=6 * EARLY * BLK * BLK * shots, bytes_accessed=12 << 20, transcendentals=0),
        name="early_tiles",
    )(pairs, place, pltpu.with_memory_space_constraint(features, pltpu.HBM))


def inside(block):
    return jnp.logical_and(block >= 0, block < OWN)


def mixed_tile(a, b, own_a, own_b, halos, tiles_ref):
    def put(left, right):
        tile = product(left[0][...], left[1][...], right[0][...], right[1][...])
        tiles_ref[...] = tile.reshape(SHARDS, 1, ROWS, BLK)

    pl.when(jnp.logical_and(inside(a), inside(b)))(lambda: put(own_a, own_b))
    for here, halo in halos:
        pl.when(jnp.logical_and(inside(a), jnp.logical_and(jnp.logical_not(inside(b)), here(b))))(lambda: put(own_a, halo))
        pl.when(jnp.logical_and(jnp.logical_not(inside(a)), here(a)))(lambda: put(halo, own_b))


def with_b_kernel(
    first_ref, second_ref, hi_a, lo_a, hi_b, lo_b, halo_ref, _, tiles_ref, hhi, hlo, unused
):
    step = pl.program_id(0)

    @pl.when(step == 0)
    def _():
        split_block(halo_ref[...], hhi, hlo, 0, unused, 0)

    slot = SLOTS_B[0] + step + jnp.where(step == 2, SLOTS_B[2] - SLOTS_B[1] - 1, 0)
    halos = [(lambda block: block == block, (hhi, hlo))]
    mixed_tile(first_ref[slot], second_ref[slot], (hi_a, lo_a), (hi_b, lo_b), halos, tiles_ref)


def with_a_kernel(
    first_ref, second_ref, place_ref, hi_a, lo_a, hi_b, lo_b, hhi, hlo, halo_ref, _, tiles_ref, ahi, alo, unused
):
    step = pl.program_id(0)

    @pl.when(step == 0)
    def _():
        split_block(halo_ref[...], ahi, alo, 0, unused, 0)

    slot = SLOTS_A[0] + step + jnp.where(step == 2, SLOTS_A[2] - SLOTS_A[1] - 1, 0)
    below_is_a = place_ref[1] == 0
    halos = [
        (lambda block: (block < 0) == below_is_a, (ahi, alo)),
        (lambda block: (block < 0) != below_is_a, (hhi, hlo)),
    ]
    mixed_tile(first_ref[slot], second_ref[slot], (hi_a, lo_a), (hi_b, lo_b), halos, tiles_ref)


SLOTS_B = (10, 11, 14)
SLOTS_A = (12, 13, 15)


def near(slots, first, second, place, hi, lo, split, halo, tiles):
    shots = hi.shape[1]
    skip = slots[2] - slots[1] - 1

    def slot_of(i):
        return slots[0] + i + jnp.where(i == 2, skip, 0)

    left = pl.BlockSpec((BLK, shots), lambda i, *s: (jnp.clip(s[0][slot_of(i)], 0, OWN - 1), 0))
    right = pl.BlockSpec((BLK, shots), lambda i, *s: (jnp.clip(s[1][slot_of(i)], 0, OWN - 1), 0))
    whole = pl.BlockSpec((BLK, shots), lambda i, *s: (0, 0))
    tile = pl.BlockSpec((SHARDS, 1, ROWS, BLK), lambda i, *s: (0, slot_of(i), 0, 0))
    parts = [jax.ShapeDtypeStruct((BLK, shots), BF16)] * 2
    vmem_parts = [pltpu.VMEM((BLK, shots), BF16)] * 2
    alone = split is None
    scalars = (first, second) if alone else (first, second, place)
    arrays = (hi, lo, hi, lo) + (() if alone else tuple(split)) + (halo, tiles)
    return pl.pallas_call(
        with_b_kernel if alone else with_a_kernel,
        grid_spec=pltpu.PrefetchScalarGridSpec(
            num_scalar_prefetch=len(scalars),
            grid=(3,),
            in_specs=[left, left, right, right]
            + ([] if alone else [whole, whole])
            + [whole, pl.BlockSpec(memory_space=pl.ANY)],
            out_specs=[tile] + ([whole, whole] if alone else []),
            scratch_shapes=([] if alone else vmem_parts) + [pltpu.VMEM((2, 8, BLK), F32)],
        ),
        out_shape=[pltpu.HBM(tiles.shape, F32)] + (parts if alone else []),
        input_output_aliases={len(scalars) + len(arrays) - 1: 0},
        compiler_params=pltpu.CompilerParams(vmem_limit_bytes=24 << 20),
        cost_estimate=pl.CostEstimate(flops=6 * 3 * BLK * BLK * shots, bytes_accessed=5 << 20, transcendentals=0),
        name="tiles_with_b" if alone else "tiles_with_a",
    )(*scalars, *arrays)


def factors_kernel(
    count, first_ref, second_ref, me_ref, own_ref, below_ref, above_ref, shift_ref, scale_ref, turned, dev, inv
):
    shards = own_ref.shape[0]
    total = shards * count
    stats = jnp.concatenate([below_ref[...], own_ref[...], above_ref[...]], axis=2)
    means, squares = stats[:, 0], stats[:, 1]
    mean = jnp.sum(means, axis=0) * (1.0 / shards)
    away = means - mean[None]
    squares = jnp.sum(squares, axis=0) + count * jnp.sum(away * away, axis=0)
    inverse = lax.rsqrt(squares * (1.0 / total) + 1e-06)
    inv[...] = inverse
    for block in range(8):
        dev[block] = away[:, block, :]
    for block in range(OWN):
        column = jnp.concatenate(
            [away[:, 2 + block, :], jnp.broadcast_to(inverse[2 + block : 3 + block, :], (128 - shards, BLK))], axis=0
        )
        turned[block] = jnp.transpose(column)
    mine = pl.ds(pl.multiple_of(me_ref[0] * ROWS, ROWS), ROWS)
    for slot in range(SLOTS):
        a = jnp.clip(first_ref[slot], 0, OWN - 1)
        b = second_ref[slot] + 2
        left = turned[a, mine, :]
        shift_ref[slot] = count * jnp.dot(
            left[:, :shards], dev[b], precision=lax.Precision.HIGHEST, preferred_element_type=F32
        )
        scale_ref[slot] = left[:, shards : shards + 1] * inv[pl.ds(b, 1), :] * (1.0 / total**0.5)


def factors(count, first, second, me, *stats):
    vmem = pl.BlockSpec(memory_space=pltpu.VMEM)
    smem = pl.BlockSpec(memory_space=SMEM)
    return pl.pallas_call(
        functools.partial(factors_kernel, count),
        in_specs=[smem] * 3 + [vmem] * 3,
        out_specs=[vmem] * 2,
        out_shape=[jax.ShapeDtypeStruct((SLOTS, ROWS, BLK), F32)] * 2,
        scratch_shapes=[
            pltpu.VMEM((OWN, BLK, 128), F32),
            pltpu.VMEM((8, SHARDS, BLK), F32),
            pltpu.VMEM((8, BLK), F32),
        ],
        compiler_params=pltpu.CompilerParams(vmem_limit_bytes=8 << 20),
        cost_estimate=pl.CostEstimate(flops=1 << 26, bytes_accessed=2 << 20, transcendentals=2048),
        name="factors",
    )(first, second, me, *stats)


def finish_kernel(slot_ref, main_ref, home_a_ref, home_b_ref, shift_ref, scale_ref, out_ref, all_ref):
    all_ref[:MADE] = (main_ref[...] + shift_ref[:MADE]) * scale_ref[:MADE]
    all_ref[HOME_A] = (home_a_ref[...] + shift_ref[HOME_A]) * scale_ref[HOME_A]
    all_ref[HOME_B] = (home_b_ref[...] + shift_ref[HOME_B]) * scale_ref[HOME_B]
    for p in range(PAIRS):
        out_ref[:, p, :] = all_ref[slot_ref[p]]


def finish(slot, main, home_a, home_b, shift, scale):
    vmem = pl.BlockSpec(memory_space=pltpu.VMEM)
    return pl.pallas_call(
        finish_kernel,
        in_specs=[pl.BlockSpec(memory_space=SMEM)] + [vmem] * 5,
        out_specs=vmem,
        out_shape=jax.ShapeDtypeStruct((ROWS, PAIRS, BLK), F32),
        scratch_shapes=[pltpu.VMEM((SLOTS, ROWS, BLK), F32)],
        compiler_params=pltpu.CompilerParams(vmem_limit_bytes=8 << 20),
        cost_estimate=pl.CostEstimate(flops=1 << 18, bytes_accessed=1 << 20, transcendentals=0),
        name="finish",
    )(slot, main, home_a, home_b, shift, scale)


def on_device(features, pairs):
    shots = features.shape[1]
    owners = lax.axis_size("det")
    owner = lax.axis_index("det").astype(jnp.int32)
    core = lax.rem(owner, 2)
    place = jnp.stack([owner * OWN, core])
    me = lax.axis_index("shot").astype(jnp.int32).reshape(1)

    def swap(x, start):
        ends = [(i, i + 1) for i in range(start, owners - 1, 2)]
        return lax.ppermute(x, "det", ends + [(b, a) for a, b in ends])

    to_a, to_b = borders(core.reshape(1), features)
    from_a = swap(to_a, 1)
    from_b = swap(to_b, 0)
    tiles, hi, lo, stats, first, second, slot = early(pairs, place, features)
    tiles, *split = near(SLOTS_B, first, second, place, hi, lo, None, from_b, tiles)
    (tiles,) = near(SLOTS_A, first, second, place, hi, lo, split, from_a, tiles)
    main = lax.psum_scatter(
        tiles.reshape(SHARDS * MADE * ROWS, BLK), "shot", scatter_dimension=0, tiled=True
    ).reshape(MADE, ROWS, BLK)

    stats, tiles = lax.optimization_barrier((stats, tiles))
    stats = lax.all_gather(stats.reshape(2 * OWN, BLK), "shot").reshape(-1, 2, OWN, BLK)
    up = [(i, i + 1) for i in range(owners - 1)]
    below = lax.ppermute(stats[:, :, 2:], "det", up)
    above = lax.ppermute(stats[:, :, :2], "det", [(b, a) for a, b in up])
    shift, scale = factors(float(shots), first, second, me, stats, below, above)
    home_a, home_b = swap(main[15], 1), swap(main[14], 0)
    return finish(slot, main, home_a, home_b, shift, scale)


def solution(mesh):
    in_specs = (P("det", "shot"), P("det", None))
    out_specs = P("shot", "det", None)
    return jax.shard_map(on_device, mesh=mesh, in_specs=in_specs, out_specs=out_specs, check_vma=False)
```

```python
import functools

import jax
import jax.numpy as jnp
from jax import lax
from jax.experimental import pallas as pl
from jax.experimental.pallas import tpu as pltpu
from jax.sharding import PartitionSpec as P

BLK = 256
OWN = 4
EARLY = 10
MADE = 16
PAIRS = 16
HOME = 16
SLOTS = 17
SHARDS = 16
ROWS = BLK // SHARDS
F32 = jnp.float32
BF16 = jnp.bfloat16
SMEM = pltpu.SMEM
VMEM = pltpu.VMEM


def split_block(x, hi_ref, lo_ref, at, stats_ref, row):
    count = x.shape[1]
    mean = jnp.sum(x, axis=1, keepdims=True) * (1.0 / count)
    centered = x - mean
    squares = jnp.sum(centered * centered, axis=1, keepdims=True)
    hi = centered.astype(BF16)
    hi_ref[pl.ds(at, BLK), :] = hi
    lo_ref[pl.ds(at, BLK), :] = (centered - hi.astype(F32)).astype(BF16)
    lane = lax.broadcasted_iota(jnp.int32, (BLK, 128), 1)
    both = jnp.where(lane < 8, jnp.broadcast_to(mean, (BLK, 128)), jnp.broadcast_to(squares, (BLK, 128)))
    flat = jnp.transpose(both)
    stats_ref[0, pl.ds(row, 1), :] = flat[0:1, :]
    stats_ref[1, pl.ds(row, 1), :] = flat[8:9, :]


def product(hi_a, lo_a, hi_b, lo_b):
    dims = (((1,), (1,)), ((), ()))
    dot = functools.partial(lax.dot_general, dimension_numbers=dims, preferred_element_type=F32)
    return dot(hi_a, hi_b) + (dot(hi_a, lo_b) + dot(lo_a, hi_b))


def borders_kernel(core_ref, x_ref, a_ref, b_ref, sems):
    core = core_ref[0]
    to_a = pltpu.make_async_copy(x_ref.at[pl.ds(core * (3 * BLK), BLK), :], a_ref, sems.at[0])
    to_b = pltpu.make_async_copy(x_ref.at[pl.ds((1 - core) * (2 * BLK), 2 * BLK), :], b_ref, sems.at[1])
    to_a.start()
    to_b.start()
    to_a.wait()
    to_b.wait()


def borders(core, features):
    shots = features.shape[1]
    return pl.pallas_call(
        borders_kernel,
        in_specs=[pl.BlockSpec(memory_space=SMEM), pl.BlockSpec(memory_space=pl.ANY)],
        out_specs=[pl.BlockSpec(memory_space=VMEM)] * 2,
        out_shape=[jax.ShapeDtypeStruct((BLK, shots), F32), jax.ShapeDtypeStruct((2 * BLK, shots), F32)],
        scratch_shapes=[pltpu.SemaphoreType.DMA((2,))],
        compiler_params=pltpu.CompilerParams(vmem_limit_bytes=8 << 20),
        cost_estimate=pl.CostEstimate(flops=0, bytes_accessed=4 << 20, transcendentals=0),
        name="borders",
    )(core, pltpu.with_memory_space_constraint(features, pltpu.HBM))


def assign(pairs_ref, base, core, first_ref, second_ref, slot_ref):
    def kind_of(p):
        second = pairs_ref[p, 1] - base
        own = jnp.logical_and(second >= 0, second < OWN)
        near = jnp.logical_and(second >= -1, second <= OWN)
        with_a = (second < 0) == (core == 0)
        return jnp.where(own, 0, jnp.where(with_a, jnp.where(near, 2, 3), 1))

    first_ref[HOME] = 0
    second_ref[HOME] = 0
    first_ref[15] = jnp.where(core == 0, -1, OWN)
    second_ref[15] = jnp.where(core == 0, 1, 2)
    kinds = [kind_of(p) for p in range(PAIRS)]
    places = [jnp.int32(0)]
    for k in range(2):
        places.append(places[-1] + sum((kind == k).astype(jnp.int32) for kind in kinds))
    for p, kind in enumerate(kinds):
        place = jnp.where(kind == 0, places[0], jnp.where(kind == 1, places[1], places[2]))
        slot = jnp.where(kind == 3, HOME, place)
        places = [place + (kind == k).astype(jnp.int32) for k, place in enumerate(places)]
        slot_ref[p] = slot
        first_ref[slot] = pairs_ref[p, 0] - base
        second_ref[slot] = pairs_ref[p, 1] - base


def fill(start, count, make, tiles_ref, buffers, sems):
    def copy(step):
        way = lax.rem(step, 2)
        return pltpu.make_async_copy(buffers.at[way], tiles_ref.at[:, start + step], sems.at[way])

    def body(step, carry):
        pl.when(step >= 2)(lambda: copy(step - 2).wait())

        def put(tile):
            buffers[lax.rem(step, 2)] = tile.reshape(SHARDS, ROWS, BLK)

        make(start + step, put)
        copy(step).start()
        return carry

    lax.fori_loop(0, count, body, 0)
    copy(jnp.int32(count - 2)).wait()
    copy(jnp.int32(count - 1)).wait()


def rows_of(ref, place):
    return ref[pl.ds(pl.multiple_of(place * BLK, BLK), BLK), :]


def early_kernel(
    pairs_ref, place_ref, x_ref, tiles_ref, hi_ref, lo_ref, stats_ref, first_ref, second_ref, slot_ref,
    x_vmem, buffers, in_sems, out_sems,
):
    loads = [
        pltpu.make_async_copy(x_ref.at[pl.ds(k * BLK, BLK), :], x_vmem.at[k], in_sems.at[k]) for k in range(OWN)
    ]
    for load in loads:
        load.start()
    assign(pairs_ref, place_ref[0], place_ref[1], first_ref, second_ref, slot_ref)
    for k, load in enumerate(loads):
        load.wait()
        split_block(x_vmem[k], hi_ref, lo_ref, k * BLK, stats_ref, k)

    def make(slot, put):
        a, b = first_ref[slot], second_ref[slot]
        put(product(rows_of(hi_ref, a), rows_of(lo_ref, a), rows_of(hi_ref, b), rows_of(lo_ref, b)))

    fill(0, EARLY, make, tiles_ref, buffers, out_sems)


def early(pairs, place, features):
    rows, shots = features.shape
    smem, vmem, anywhere = (pl.BlockSpec(memory_space=space) for space in (SMEM, VMEM, pl.ANY))
    return pl.pallas_call(
        early_kernel,
        in_specs=[smem, smem, anywhere],
        out_specs=[anywhere, vmem, vmem, vmem, smem, smem, smem],
        out_shape=[
            pltpu.HBM((SHARDS, MADE, ROWS, BLK), F32),
            jax.ShapeDtypeStruct((rows, shots), BF16),
            jax.ShapeDtypeStruct((rows, shots), BF16),
            jax.ShapeDtypeStruct((2, OWN, BLK), F32),
            jax.ShapeDtypeStruct((SLOTS,), jnp.int32),
            jax.ShapeDtypeStruct((SLOTS,), jnp.int32),
            jax.ShapeDtypeStruct((PAIRS,), jnp.int32),
        ],
        scratch_shapes=[
            VMEM((OWN, BLK, shots), F32),
            VMEM((2, SHARDS, ROWS, BLK), F32),
            pltpu.SemaphoreType.DMA((OWN,)),
            pltpu.SemaphoreType.DMA((2,)),
        ],
        compiler_params=pltpu.CompilerParams(vmem_limit_bytes=24 << 20),
        cost_estimate=pl.CostEstimate(flops=6 * EARLY * BLK * BLK * shots, bytes_accessed=12 << 20, transcendentals=0),
        name="early_tiles",
    )(pairs, place, pltpu.with_memory_space_constraint(features, pltpu.HBM))


def mixed(first_ref, second_ref, own, halos):
    def inside(block):
        return jnp.logical_and(block >= 0, block < OWN)

    def parts(refs, place):
        return [rows_of(ref, place) for ref in refs]

    def make(slot, put):
        a, b = first_ref[slot], second_ref[slot]
        a_in, b_in = inside(a), inside(b)
        pl.when(jnp.logical_and(a_in, b_in))(lambda: put(product(*parts(own, a), *parts(own, b))))
        for here, place, halo in halos:

            @pl.when(jnp.logical_and(jnp.logical_not(b_in), here(b)))
            def _():
                put(product(*parts(own, a), *parts(halo, place(b))))

            @pl.when(jnp.logical_and(jnp.logical_not(a_in), here(a)))
            def _():
                put(product(*parts(halo, place(a)), *parts(own, b)))

    return make


def place_in_b(block):
    return jnp.where(block < 0, block + 2, block - OWN)


def with_b_kernel(
    first_ref, second_ref, hi_ref, lo_ref, halo_ref, _, tiles_ref, bhi_ref, blo_ref, unused, buffers, sems
):
    for k in range(2):
        split_block(halo_ref[k * BLK : (k + 1) * BLK, :], bhi_ref, blo_ref, k * BLK, unused, k)
    halos = [(lambda block: block == block, place_in_b, (bhi_ref, blo_ref))]
    make = mixed(first_ref, second_ref, (hi_ref, lo_ref), halos)
    fill(EARLY, 3, make, tiles_ref, buffers, sems)


def with_a_kernel(
    first_ref, second_ref, place_ref, hi_ref, lo_ref, bhi_ref, blo_ref, halo_ref, _, tiles_ref,
    ahi_ref, alo_ref, unused, buffers, sems,
):
    split_block(halo_ref[...], ahi_ref, alo_ref, 0, unused, 0)
    below_is_a = place_ref[1] == 0
    halos = [
        (lambda block: (block < 0) == below_is_a, lambda block: 0, (ahi_ref, alo_ref)),
        (lambda block: (block < 0) != below_is_a, place_in_b, (bhi_ref, blo_ref)),
    ]
    make = mixed(first_ref, second_ref, (hi_ref, lo_ref), halos)
    fill(EARLY + 3, 3, make, tiles_ref, buffers, sems)


def near(kernel, scalars, arrays, tiles, split_out, shots, name):
    smem, vmem, anywhere = (pl.BlockSpec(memory_space=space) for space in (SMEM, VMEM, pl.ANY))
    ahead = len(scalars) + len(arrays)
    return pl.pallas_call(
        kernel,
        in_specs=[smem] * len(scalars) + [vmem] * len(arrays) + [anywhere],
        out_specs=[anywhere] + ([vmem] * 2 if split_out else []),
        out_shape=[pltpu.HBM(tiles.shape, F32)]
        + ([jax.ShapeDtypeStruct((split_out * BLK, shots), BF16)] * 2 if split_out else []),
        scratch_shapes=([] if split_out else [VMEM((BLK, shots), BF16)] * 2)
        + [VMEM((2, 8, BLK), F32), VMEM((2, SHARDS, ROWS, BLK), F32), pltpu.SemaphoreType.DMA((2,))],
        input_output_aliases={ahead: 0},
        compiler_params=pltpu.CompilerParams(vmem_limit_bytes=16 << 20),
        cost_estimate=pl.CostEstimate(flops=6 * 3 * BLK * BLK * shots, bytes_accessed=5 << 20, transcendentals=0),
        name=name,
    )(*scalars, *arrays, tiles)


def factors_kernel(
    count, first_ref, second_ref, me_ref, own_ref, below_ref, above_ref, shift_ref, scale_ref, turned, dev, inv
):
    shards = own_ref.shape[0]
    total = shards * count
    stats = jnp.concatenate([below_ref[...], own_ref[...], above_ref[...]], axis=2)
    means, squares = stats[:, 0], stats[:, 1]
    mean = jnp.sum(means, axis=0) * (1.0 / shards)
    away = means - mean[None]
    squares = jnp.sum(squares, axis=0) + count * jnp.sum(away * away, axis=0)
    inverse = lax.rsqrt(squares * (1.0 / total) + 1e-06)
    inv[...] = inverse
    for block in range(8):
        dev[block] = away[:, block, :]
    for block in range(OWN):
        column = jnp.concatenate(
            [away[:, 2 + block, :], jnp.broadcast_to(inverse[2 + block : 3 + block, :], (128 - shards, BLK))], axis=0
        )
        turned[block] = jnp.transpose(column)
    mine = pl.ds(pl.multiple_of(me_ref[0] * ROWS, ROWS), ROWS)
    for slot in range(SLOTS):
        a = jnp.clip(first_ref[slot], 0, OWN - 1)
        b = second_ref[slot] + 2
        left = turned[a, mine, :]
        shift_ref[slot] = count * jnp.dot(
            left[:, :shards], dev[b], precision=lax.Precision.HIGHEST, preferred_element_type=F32
        )
        scale_ref[slot] = left[:, shards : shards + 1] * inv[pl.ds(b, 1), :] * (1.0 / total**0.5)


def factors(count, first, second, me, *stats):
    vmem = pl.BlockSpec(memory_space=VMEM)
    smem = pl.BlockSpec(memory_space=SMEM)
    return pl.pallas_call(
        functools.partial(factors_kernel, count),
        in_specs=[smem] * 3 + [vmem] * 3,
        out_specs=[vmem] * 2,
        out_shape=[jax.ShapeDtypeStruct((SLOTS, ROWS, BLK), F32)] * 2,
        scratch_shapes=[
            VMEM((OWN, BLK, 128), F32),
            VMEM((8, SHARDS, BLK), F32),
            VMEM((8, BLK), F32),
        ],
        compiler_params=pltpu.CompilerParams(vmem_limit_bytes=8 << 20),
        cost_estimate=pl.CostEstimate(flops=1 << 26, bytes_accessed=2 << 20, transcendentals=2048),
        name="factors",
    )(first, second, me, *stats)


def finish_kernel(slot_ref, main_ref, home_ref, shift_ref, scale_ref, out_ref, all_ref):
    all_ref[:MADE] = (main_ref[...] + shift_ref[:MADE]) * scale_ref[:MADE]
    all_ref[HOME] = (home_ref[...] + shift_ref[HOME]) * scale_ref[HOME]
    for p in range(PAIRS):
        out_ref[:, p, :] = all_ref[slot_ref[p]]


def finish(slot, main, home, shift, scale):
    vmem = pl.BlockSpec(memory_space=VMEM)
    return pl.pallas_call(
        finish_kernel,
        in_specs=[pl.BlockSpec(memory_space=SMEM)] + [vmem] * 4,
        out_specs=vmem,
        out_shape=jax.ShapeDtypeStruct((ROWS, PAIRS, BLK), F32),
        scratch_shapes=[VMEM((SLOTS, ROWS, BLK), F32)],
        compiler_params=pltpu.CompilerParams(vmem_limit_bytes=8 << 20),
        cost_estimate=pl.CostEstimate(flops=1 << 18, bytes_accessed=1 << 20, transcendentals=0),
        name="finish",
    )(slot, main, home, shift, scale)


def on_device(features, pairs):
    shots = features.shape[1]
    owners = lax.axis_size("det")
    owner = lax.axis_index("det").astype(jnp.int32)
    core = lax.rem(owner, 2)
    place = jnp.stack([owner * OWN, core])
    me = lax.axis_index("shot").astype(jnp.int32).reshape(1)

    def swap(x, start):
        ends = [(i, i + 1) for i in range(start, owners - 1, 2)]
        return lax.ppermute(x, "det", ends + [(b, a) for a, b in ends])

    to_a, to_b = borders(core.reshape(1), features)
    from_a = swap(to_a, 1)
    from_b = swap(to_b, 0)
    tiles, hi, lo, stats, first, second, slot = early(pairs, place, features)
    tiles, *split = near(with_b_kernel, (first, second), (hi, lo, from_b), tiles, 2, shots, "tiles_with_b")
    (tiles,) = near(with_a_kernel, (first, second, place), (hi, lo, *split, from_a), tiles, 0, shots, "tiles_with_a")
    main = lax.psum_scatter(
        tiles.reshape(SHARDS * MADE * ROWS, BLK), "shot", scatter_dimension=0, tiled=True
    ).reshape(MADE, ROWS, BLK)

    stats, tiles = lax.optimization_barrier((stats, tiles))
    stats = lax.all_gather(stats.reshape(2 * OWN, BLK), "shot").reshape(-1, 2, OWN, BLK)
    up = [(i, i + 1) for i in range(owners - 1)]
    below = lax.ppermute(stats[:, :, 2:], "det", up)
    above = lax.ppermute(stats[:, :, :2], "det", [(b, a) for a, b in up])
    shift, scale = factors(float(shots), first, second, me, stats, below, above)
    return finish(slot, main, swap(main[15], 1), shift, scale)


def solution(mesh):
    in_specs = (P("det", "shot"), P("det", None))
    out_specs = P("shot", "det", None)
    return jax.shard_map(on_device, mesh=mesh, in_specs=in_specs, out_specs=out_specs, check_vma=False)
```

```python
import functools

import jax
import jax.numpy as jnp
from jax import lax
from jax.experimental import pallas as pl
from jax.experimental.pallas import tpu as pltpu
from jax.sharding import PartitionSpec as P

BLK = 256
OWN = 4
EARLY = 10
MADE = 16
PAIRS = 16
HOME = 16
SLOTS = 17
PLACES = 7
AT_ONCE = 10
COST = 1 << 34
SHARDS = 16
ROWS = BLK // SHARDS
F32 = jnp.float32
BF16 = jnp.bfloat16
SMEM = pltpu.SMEM
VMEM = pltpu.VMEM


def split_block(x, parts_ref, place, stats_ref, row):
    count = x.shape[1]
    mean = jnp.sum(x, axis=1, keepdims=True) * (1.0 / count)
    centered = x - mean
    hi = centered.astype(BF16)
    at = 2 * BLK * place
    parts_ref[at : at + BLK, :] = hi
    parts_ref[at + BLK : at + 2 * BLK, :] = (centered - hi.astype(F32)).astype(BF16)
    if stats_ref is None:
        return
    squares = jnp.sum(centered * centered, axis=1, keepdims=True)
    lane = lax.broadcasted_iota(jnp.int32, (BLK, 128), 1)
    both = jnp.where(lane < 8, jnp.broadcast_to(mean, (BLK, 128)), jnp.broadcast_to(squares, (BLK, 128)))
    flat = jnp.transpose(both)
    stats_ref[0, pl.ds(row, 1), :] = flat[0:1, :]
    stats_ref[1, pl.ds(row, 1), :] = flat[8:9, :]


def product(parts_ref, a, b):
    dot = functools.partial(
        lax.dot_general, dimension_numbers=(((1,), (1,)), ((), ())), preferred_element_type=F32
    )
    at = pl.multiple_of(a * (2 * BLK), 2 * BLK)
    by = pl.multiple_of(b * (2 * BLK), 2 * BLK)
    both = dot(parts_ref[pl.ds(at, 2 * BLK), :], parts_ref[pl.ds(by, BLK), :])
    rest = dot(parts_ref[pl.ds(at, BLK), :], parts_ref[pl.ds(by + BLK, BLK), :])
    return both[:BLK] + (both[BLK:] + rest)


def border_kernel(start_ref, x_ref, out_ref, sem):
    copy = pltpu.make_async_copy(x_ref.at[pl.ds(start_ref[0] * BLK, out_ref.shape[0]), :], out_ref, sem)
    copy.start()
    copy.wait()


def border(start, blocks, features, name):
    shots = features.shape[1]
    return pl.pallas_call(
        border_kernel,
        in_specs=[pl.BlockSpec(memory_space=SMEM), pl.BlockSpec(memory_space=pl.ANY)],
        out_specs=pl.BlockSpec(memory_space=VMEM),
        out_shape=jax.ShapeDtypeStruct((blocks * BLK, shots), F32),
        scratch_shapes=[pltpu.SemaphoreType.DMA],
        compiler_params=pltpu.CompilerParams(vmem_limit_bytes=8 << 20),
        cost_estimate=pl.CostEstimate(flops=0, bytes_accessed=blocks << 21, transcendentals=0),
        name=name,
    )(start.reshape(1), pltpu.with_memory_space_constraint(features, pltpu.HBM))


def assign(pairs_ref, base, core, first_ref, second_ref, slot_ref, left_ref, right_ref):
    def kind_of(p):
        second = pairs_ref[p, 1] - base
        own = jnp.logical_and(second >= 0, second < OWN)
        near = jnp.logical_and(second >= -1, second <= OWN)
        with_a = (second < 0) == (core == 0)
        return jnp.where(own, 0, jnp.where(with_a, jnp.where(near, 2, 3), 1))

    first_ref[HOME] = 0
    second_ref[HOME] = 0
    first_ref[15] = jnp.where(core == 0, -1, OWN)
    second_ref[15] = jnp.where(core == 0, 1, 2)
    kinds = [kind_of(p) for p in range(PAIRS)]
    n_in, n_with_b = (sum((kind == k).astype(jnp.int32) for kind in kinds) for k in range(2))
    places = [jnp.int32(0), jnp.int32(EARLY), n_in + n_with_b]
    for p, kind in enumerate(kinds):
        own = places[0] + jnp.where(places[0] >= EARLY, n_with_b, 0)
        place = jnp.where(kind == 0, own, jnp.where(kind == 1, places[1], places[2]))
        slot = jnp.where(kind == 3, HOME, place)
        places = [place + (kind == k).astype(jnp.int32) for k, place in enumerate(places)]
        slot_ref[p] = slot
        first_ref[slot] = pairs_ref[p, 0] - base
        second_ref[slot] = pairs_ref[p, 1] - base

    def place_of(block):
        with_a = (block < 0) == (core == 0)
        beside = jnp.where(with_a, 6, jnp.where(block < 0, block + 6, block))
        return jnp.where(jnp.logical_and(block >= 0, block < OWN), block, beside)

    for slot in range(MADE):
        left_ref[slot] = place_of(first_ref[slot])
        right_ref[slot] = place_of(second_ref[slot])


def fill(start, count, at_once, parts_ref, left_ref, right_ref, tiles_ref, buffers, sems):
    rounds = count // at_once

    def copy(step, k):
        way = lax.rem(step, 2) * at_once + k if rounds > 1 else k
        return pltpu.make_async_copy(buffers.at[way], tiles_ref.at[:, start + step * at_once + k], sems.at[way])

    def body(step, carry):
        slots = [start + step * at_once + k for k in range(at_once)]
        tiles = [product(parts_ref, left_ref[slot], right_ref[slot]) for slot in slots]
        for k, tile in enumerate(tiles):
            pl.when(step >= 2)(lambda: copy(step - 2, k).wait())
            buffers[lax.rem(step, 2) * at_once + k if rounds > 1 else k] = tile.reshape(SHARDS, ROWS, BLK)
            copy(step, k).start()
        return carry

    lax.fori_loop(0, rounds, body, 0)
    for step in range(max(rounds - 2, 0), rounds):
        for k in range(at_once):
            copy(jnp.int32(step), k).wait()


def early_kernel(
    pairs_ref, place_ref, x_ref, tiles_ref, parts_ref, stats_ref, first_ref, second_ref, slot_ref, left_ref, right_ref,
    x_vmem, buffers, in_sems, out_sems,
):
    loads = [
        pltpu.make_async_copy(x_ref.at[pl.ds(k * BLK, BLK), :], x_vmem.at[k], in_sems.at[k]) for k in range(OWN)
    ]
    for load in loads:
        load.start()
    assign(pairs_ref, place_ref[0], place_ref[1], first_ref, second_ref, slot_ref, left_ref, right_ref)
    for k, load in enumerate(loads):
        load.wait()
        split_block(x_vmem[k], parts_ref, k, stats_ref, k)
    fill(0, EARLY, AT_ONCE, parts_ref, left_ref, right_ref, tiles_ref, buffers, out_sems)


def early(pairs, place, features):
    shots = features.shape[1]
    smem, vmem, anywhere = (pl.BlockSpec(memory_space=space) for space in (SMEM, VMEM, pl.ANY))
    numbers = jax.ShapeDtypeStruct((SLOTS,), jnp.int32)
    return pl.pallas_call(
        early_kernel,
        in_specs=[smem, smem, anywhere],
        out_specs=[anywhere, vmem, vmem] + [smem] * 5,
        out_shape=[
            pltpu.HBM((SHARDS, MADE, ROWS, BLK), F32),
            jax.ShapeDtypeStruct((PLACES * 2 * BLK, shots), BF16),
            jax.ShapeDtypeStruct((2, OWN, BLK), F32),
            numbers,
            numbers,
            jax.ShapeDtypeStruct((PAIRS,), jnp.int32),
            numbers,
            numbers,
        ],
        scratch_shapes=[
            VMEM((OWN, BLK, shots), F32),
            VMEM((AT_ONCE, SHARDS, ROWS, BLK), F32),
            pltpu.SemaphoreType.DMA((OWN,)),
            pltpu.SemaphoreType.DMA((AT_ONCE,)),
        ],
        compiler_params=pltpu.CompilerParams(vmem_limit_bytes=24 << 20),
        cost_estimate=pl.CostEstimate(flops=6 * EARLY * BLK * BLK * shots, bytes_accessed=12 << 20, transcendentals=0),
        name="early_tiles",
    )(pairs, place, pltpu.with_memory_space_constraint(features, pltpu.HBM))


def near_kernel(start, place, left_ref, right_ref, halo_ref, _, __, tiles_ref, parts_ref, buffers, sems):
    for k in range(halo_ref.shape[0] // BLK):
        split_block(halo_ref[k * BLK : (k + 1) * BLK, :], parts_ref, place + k, None, None)
    fill(start, 3, 3, parts_ref, left_ref, right_ref, tiles_ref, buffers, sems)


def near(start, place, left, right, halo, parts, tiles, name, cost):
    smem, vmem, anywhere = (pl.BlockSpec(memory_space=space) for space in (SMEM, VMEM, pl.ANY))
    return pl.pallas_call(
        functools.partial(near_kernel, start, place),
        in_specs=[smem, smem, vmem, vmem, anywhere],
        out_specs=[anywhere, vmem],
        out_shape=[pltpu.HBM(tiles.shape, F32), jax.ShapeDtypeStruct(parts.shape, BF16)],
        scratch_shapes=[VMEM((3, SHARDS, ROWS, BLK), F32), pltpu.SemaphoreType.DMA((3,))],
        input_output_aliases={3: 1, 4: 0},
        compiler_params=pltpu.CompilerParams(vmem_limit_bytes=16 << 20),
        cost_estimate=pl.CostEstimate(flops=cost, bytes_accessed=1 << 20, transcendentals=0),
        name=name,
    )(left, right, halo, parts, tiles)


def factors_kernel(
    count, first_ref, second_ref, me_ref, own_ref, below_ref, above_ref, shift_ref, scale_ref, turned, dev, inv
):
    shards = own_ref.shape[0]
    total = shards * count
    stats = jnp.concatenate([below_ref[...], own_ref[...], above_ref[...]], axis=2)
    means, squares = stats[:, 0], stats[:, 1]
    mean = jnp.sum(means, axis=0) * (1.0 / shards)
    away = means - mean[None]
    squares = jnp.sum(squares, axis=0) + count * jnp.sum(away * away, axis=0)
    inverse = lax.rsqrt(squares * (1.0 / total) + 1e-06)
    inv[...] = inverse
    for block in range(8):
        dev[block] = away[:, block, :]
    for block in range(OWN):
        column = jnp.concatenate(
            [away[:, 2 + block, :], jnp.broadcast_to(inverse[2 + block : 3 + block, :], (128 - shards, BLK))], axis=0
        )
        turned[block] = jnp.transpose(column)
    mine = pl.ds(pl.multiple_of(me_ref[0] * ROWS, ROWS), ROWS)
    for slot in range(SLOTS):
        a = jnp.clip(first_ref[slot], 0, OWN - 1)
        b = second_ref[slot] + 2
        left = turned[a, mine, :]
        shift_ref[slot] = count * jnp.dot(
            left[:, :shards], dev[b], precision=lax.Precision.HIGHEST, preferred_element_type=F32
        )
        scale_ref[slot] = left[:, shards : shards + 1] * inv[pl.ds(b, 1), :] * (1.0 / total**0.5)


def factors(count, first, second, me, *stats):
    vmem = pl.BlockSpec(memory_space=VMEM)
    smem = pl.BlockSpec(memory_space=SMEM)
    return pl.pallas_call(
        functools.partial(factors_kernel, count),
        in_specs=[smem] * 3 + [vmem] * 3,
        out_specs=[vmem] * 2,
        out_shape=[jax.ShapeDtypeStruct((SLOTS, ROWS, BLK), F32)] * 2,
        scratch_shapes=[
            VMEM((OWN, BLK, 128), F32),
            VMEM((8, SHARDS, BLK), F32),
            VMEM((8, BLK), F32),
        ],
        compiler_params=pltpu.CompilerParams(vmem_limit_bytes=8 << 20),
        cost_estimate=pl.CostEstimate(flops=1 << 26, bytes_accessed=2 << 20, transcendentals=2048),
        name="factors",
    )(first, second, me, *stats)


def finish_kernel(slot_ref, main_ref, home_ref, shift_ref, scale_ref, out_ref, all_ref):
    all_ref[:MADE] = (main_ref[...] + shift_ref[:MADE]) * scale_ref[:MADE]
    all_ref[HOME] = (home_ref[...] + shift_ref[HOME]) * scale_ref[HOME]
    for p in range(PAIRS):
        out_ref[:, p, :] = all_ref[slot_ref[p]]


def finish(slot, main, home, shift, scale):
    vmem = pl.BlockSpec(memory_space=VMEM)
    return pl.pallas_call(
        finish_kernel,
        in_specs=[pl.BlockSpec(memory_space=SMEM)] + [vmem] * 4,
        out_specs=vmem,
        out_shape=jax.ShapeDtypeStruct((ROWS, PAIRS, BLK), F32),
        scratch_shapes=[VMEM((SLOTS, ROWS, BLK), F32)],
        compiler_params=pltpu.CompilerParams(vmem_limit_bytes=8 << 20),
        cost_estimate=pl.CostEstimate(flops=1 << 18, bytes_accessed=1 << 20, transcendentals=0),
        name="finish",
    )(slot, main, home, shift, scale)


def on_device(features, pairs):
    shots = features.shape[1]
    owners = lax.axis_size("det")
    owner = lax.axis_index("det").astype(jnp.int32)
    core = lax.rem(owner, 2)
    place = jnp.stack([owner * OWN, core])
    me = lax.axis_index("shot").astype(jnp.int32).reshape(1)

    def swap(x, start):
        ends = [(i, i + 1) for i in range(start, owners - 1, 2)]
        return lax.ppermute(x, "det", ends + [(b, a) for a, b in ends])

    to_a = border(3 * core, 1, features, "border_for_a")
    later, to_a = lax.optimization_barrier((2 - 2 * core, to_a))
    from_a = swap(to_a, 1)
    from_b = swap(border(later, 2, features, "border_for_b"), 0)
    tiles, parts, stats, first, second, slot, left, right = early(pairs, place, features)
    tiles, parts = near(EARLY + 3, 6, left, right, from_a, parts, tiles, "tiles_with_a", COST)
    tiles, _ = near(EARLY, 4, left, right, from_b, parts, tiles, "tiles_with_b", COST)
    main = lax.psum_scatter(
        tiles.reshape(SHARDS * MADE * ROWS, BLK), "shot", scatter_dimension=0, tiled=True
    ).reshape(MADE, ROWS, BLK)

    stats, tiles = lax.optimization_barrier((stats, tiles))
    stats = lax.all_gather(stats.reshape(2 * OWN, BLK), "shot").reshape(-1, 2, OWN, BLK)
    up = [(i, i + 1) for i in range(owners - 1)]
    below = lax.ppermute(stats[:, :, 2:], "det", up)
    above = lax.ppermute(stats[:, :, :2], "det", [(b, a) for a, b in up])
    shift, scale = factors(float(shots), first, second, me, stats, below, above)
    return finish(slot, main, swap(main[15], 1), shift, scale)


def solution(mesh):
    in_specs = (P("det", "shot"), P("det", None))
    out_specs = P("shot", "det", None)
    return jax.shard_map(on_device, mesh=mesh, in_specs=in_specs, out_specs=out_specs, check_vma=False)
```

```python
import functools

import jax
import jax.numpy as jnp
from jax import lax
from jax.experimental import pallas as pl
from jax.experimental.pallas import tpu as pltpu
from jax.sharding import PartitionSpec as P

BLK = 256
OWN = 4
EARLY = 10
MADE = 16
PAIRS = 16
HOME = 16
SLOTS = 17
PLACES = 7
EARLY_GROUPS = (4, 3, 3)
NEAR_GROUPS = (3, 3)
SPLIT_COST = 1 << 34
SHARDS = 16
ROWS = BLK // SHARDS
F32 = jnp.float32
BF16 = jnp.bfloat16
SMEM = pltpu.SMEM
VMEM = pltpu.VMEM


def split_block(x, parts_ref, place, stats_ref, row):
    count = x.shape[1]
    mean = jnp.sum(x, axis=1, keepdims=True) * (1.0 / count)
    centered = x - mean
    hi = centered.astype(BF16)
    at = 2 * BLK * place
    parts_ref[at : at + BLK, :] = hi
    parts_ref[at + BLK : at + 2 * BLK, :] = (centered - hi.astype(F32)).astype(BF16)
    if stats_ref is None:
        return
    squares = jnp.sum(centered * centered, axis=1, keepdims=True)
    lane = lax.broadcasted_iota(jnp.int32, (BLK, 128), 1)
    both = jnp.where(lane < 8, jnp.broadcast_to(mean, (BLK, 128)), jnp.broadcast_to(squares, (BLK, 128)))
    flat = jnp.transpose(both)
    stats_ref[0, pl.ds(row, 1), :] = flat[0:1, :]
    stats_ref[1, pl.ds(row, 1), :] = flat[8:9, :]


def product(parts_ref, a, b):
    dot = functools.partial(
        lax.dot_general, dimension_numbers=(((1,), (1,)), ((), ())), preferred_element_type=F32
    )
    at = pl.multiple_of(a * (2 * BLK), 2 * BLK)
    by = pl.multiple_of(b * (2 * BLK), 2 * BLK)
    both = dot(parts_ref[pl.ds(at, 2 * BLK), :], parts_ref[pl.ds(by, BLK), :])
    rest = dot(parts_ref[pl.ds(at, BLK), :], parts_ref[pl.ds(by + BLK, BLK), :])
    return both[:BLK] + (both[BLK:] + rest)


def border_kernel(start_ref, x_ref, out_ref, held, in_sems, out_sems):
    rows = held.shape[1]
    loads, stores = [], []
    for k in range(held.shape[0]):
        here = pl.ds(pl.multiple_of(start_ref[0] * BLK + k * rows, rows), rows)
        loads.append(pltpu.make_async_copy(x_ref.at[here, :], held.at[k], in_sems.at[k]))
        stores.append(pltpu.make_async_copy(held.at[k], out_ref.at[pl.ds(k * rows, rows), :], out_sems.at[k]))
        loads[k].start()
    for load, store in zip(loads, stores):
        load.wait()
        store.start()
    for store in stores:
        store.wait()


def border(start, blocks, features, name):
    shots = features.shape[1]
    pieces = 4
    return pl.pallas_call(
        border_kernel,
        in_specs=[pl.BlockSpec(memory_space=SMEM), pl.BlockSpec(memory_space=pl.ANY)],
        out_specs=pl.BlockSpec(memory_space=pl.ANY),
        out_shape=pltpu.HBM((blocks * BLK, shots), F32),
        scratch_shapes=[
            VMEM((pieces, blocks * BLK // pieces, shots), F32),
            pltpu.SemaphoreType.DMA((pieces,)),
            pltpu.SemaphoreType.DMA((pieces,)),
        ],
        compiler_params=pltpu.CompilerParams(vmem_limit_bytes=8 << 20),
        cost_estimate=pl.CostEstimate(flops=0, bytes_accessed=blocks << 21, transcendentals=0),
        name=name,
    )(start.reshape(1), pltpu.with_memory_space_constraint(features, pltpu.HBM))


def assign(pairs_ref, base, core, first_ref, second_ref, slot_ref, left_ref, right_ref):
    def kind_of(p):
        second = pairs_ref[p, 1] - base
        own = jnp.logical_and(second >= 0, second < OWN)
        near = jnp.logical_and(second >= -1, second <= OWN)
        with_a = (second < 0) == (core == 0)
        return jnp.where(own, 0, jnp.where(with_a, jnp.where(near, 2, 3), 1))

    first_ref[HOME] = 0
    second_ref[HOME] = 0
    first_ref[15] = jnp.where(core == 0, -1, OWN)
    second_ref[15] = jnp.where(core == 0, 1, 2)
    kinds = [kind_of(p) for p in range(PAIRS)]
    n_in, n_with_b = (sum((kind == k).astype(jnp.int32) for kind in kinds) for k in range(2))
    places = [jnp.int32(0), jnp.int32(EARLY), n_in + n_with_b]
    for p, kind in enumerate(kinds):
        own = places[0] + jnp.where(places[0] >= EARLY, n_with_b, 0)
        place = jnp.where(kind == 0, own, jnp.where(kind == 1, places[1], places[2]))
        slot = jnp.where(kind == 3, HOME, place)
        places = [place + (kind == k).astype(jnp.int32) for k, place in enumerate(places)]
        slot_ref[p] = slot
        first_ref[slot] = pairs_ref[p, 0] - base
        second_ref[slot] = pairs_ref[p, 1] - base

    def place_of(block):
        with_a = (block < 0) == (core == 0)
        beside = jnp.where(with_a, 6, jnp.where(block < 0, block + 6, block))
        return jnp.where(jnp.logical_and(block >= 0, block < OWN), block, beside)

    for slot in range(MADE):
        left_ref[slot] = place_of(first_ref[slot])
        right_ref[slot] = place_of(second_ref[slot])


def fill(start, counts, parts_ref, left_ref, right_ref, tiles_ref, buffers, sems):
    def copy(k):
        return pltpu.make_async_copy(buffers.at[k], tiles_ref.at[:, start + k], sems.at[k])

    done = 0
    for count in counts:
        group = range(done, done + count)
        tiles = [product(parts_ref, left_ref[start + k], right_ref[start + k]) for k in group]
        for k, tile in zip(group, tiles):
            buffers[k] = tile.reshape(SHARDS, ROWS, BLK)
            copy(k).start()
        done += count
    for k in range(done):
        copy(k).wait()


def early_kernel(
    pairs_ref, place_ref, x_ref, tiles_ref, parts_ref, stats_ref, first_ref, second_ref, slot_ref, left_ref, right_ref,
    x_vmem, buffers, in_sems, out_sems,
):
    loads = [
        pltpu.make_async_copy(x_ref.at[pl.ds(k * BLK, BLK), :], x_vmem.at[k], in_sems.at[k]) for k in range(OWN)
    ]
    for load in loads:
        load.start()
    assign(pairs_ref, place_ref[0], place_ref[1], first_ref, second_ref, slot_ref, left_ref, right_ref)
    for k, load in enumerate(loads):
        load.wait()
        split_block(x_vmem[k], parts_ref, k, stats_ref, k)
    fill(0, EARLY_GROUPS, parts_ref, left_ref, right_ref, tiles_ref, buffers, out_sems)


def early(pairs, place, features):
    shots = features.shape[1]
    smem, vmem, anywhere = (pl.BlockSpec(memory_space=space) for space in (SMEM, VMEM, pl.ANY))
    numbers = jax.ShapeDtypeStruct((SLOTS,), jnp.int32)
    return pl.pallas_call(
        early_kernel,
        in_specs=[smem, smem, anywhere],
        out_specs=[anywhere, vmem, vmem] + [smem] * 5,
        out_shape=[
            pltpu.HBM((SHARDS, MADE, ROWS, BLK), F32),
            jax.ShapeDtypeStruct((PLACES * 2 * BLK, shots), BF16),
            jax.ShapeDtypeStruct((2, OWN, BLK), F32),
            numbers,
            numbers,
            jax.ShapeDtypeStruct((PAIRS,), jnp.int32),
            numbers,
            numbers,
        ],
        scratch_shapes=[
            VMEM((OWN, BLK, shots), F32),
            VMEM((EARLY, SHARDS, ROWS, BLK), F32),
            pltpu.SemaphoreType.DMA((OWN,)),
            pltpu.SemaphoreType.DMA((EARLY,)),
        ],
        compiler_params=pltpu.CompilerParams(vmem_limit_bytes=24 << 20),
        cost_estimate=pl.CostEstimate(flops=6 * EARLY * BLK * BLK * shots, bytes_accessed=12 << 20, transcendentals=0),
        name="early_tiles",
    )(pairs, place, pltpu.with_memory_space_constraint(features, pltpu.HBM))


def split_kernel(place, halo_ref, _, parts_ref):
    split_block(halo_ref[...], parts_ref, place, None, None)


def split(place, halo, parts):
    vmem = pl.BlockSpec(memory_space=VMEM)
    return pl.pallas_call(
        functools.partial(split_kernel, place),
        in_specs=[vmem, vmem],
        out_specs=vmem,
        out_shape=jax.ShapeDtypeStruct(parts.shape, BF16),
        input_output_aliases={1: 0},
        compiler_params=pltpu.CompilerParams(vmem_limit_bytes=8 << 20),
        cost_estimate=pl.CostEstimate(flops=SPLIT_COST, bytes_accessed=1 << 20, transcendentals=0),
        name="split_a",
    )(halo, parts)


def near_kernel(left_ref, right_ref, halo_ref, _, __, tiles_ref, parts_ref, buffers, sems):
    for k in range(2):
        split_block(halo_ref[k * BLK : (k + 1) * BLK, :], parts_ref, OWN + k, None, None)
    fill(EARLY, NEAR_GROUPS, parts_ref, left_ref, right_ref, tiles_ref, buffers, sems)


def near(left, right, halo, parts, tiles):
    smem, vmem, anywhere = (pl.BlockSpec(memory_space=space) for space in (SMEM, VMEM, pl.ANY))
    count = MADE - EARLY
    return pl.pallas_call(
        near_kernel,
        in_specs=[smem, smem, vmem, vmem, anywhere],
        out_specs=[anywhere, vmem],
        out_shape=[pltpu.HBM(tiles.shape, F32), jax.ShapeDtypeStruct(parts.shape, BF16)],
        scratch_shapes=[VMEM((count, SHARDS, ROWS, BLK), F32), pltpu.SemaphoreType.DMA((count,))],
        input_output_aliases={3: 1, 4: 0},
        compiler_params=pltpu.CompilerParams(vmem_limit_bytes=16 << 20),
        cost_estimate=pl.CostEstimate(
            flops=6 * count * BLK * BLK * halo.shape[1], bytes_accessed=5 << 20, transcendentals=0
        ),
        name="near_tiles",
    )(left, right, halo, parts, tiles)


def factors_kernel(
    count, first_ref, second_ref, me_ref, own_ref, below_ref, above_ref, shift_ref, scale_ref, turned, dev, inv
):
    shards = own_ref.shape[0]
    total = shards * count
    stats = jnp.concatenate([below_ref[...], own_ref[...], above_ref[...]], axis=2)
    means, squares = stats[:, 0], stats[:, 1]
    mean = jnp.sum(means, axis=0) * (1.0 / shards)
    away = means - mean[None]
    squares = jnp.sum(squares, axis=0) + count * jnp.sum(away * away, axis=0)
    inverse = lax.rsqrt(squares * (1.0 / total) + 1e-06)
    inv[...] = inverse
    for block in range(8):
        dev[block] = away[:, block, :]
    for block in range(OWN):
        column = jnp.concatenate(
            [away[:, 2 + block, :], jnp.broadcast_to(inverse[2 + block : 3 + block, :], (128 - shards, BLK))], axis=0
        )
        turned[block] = jnp.transpose(column)
    mine = pl.ds(pl.multiple_of(me_ref[0] * ROWS, ROWS), ROWS)
    for slot in range(SLOTS):
        a = jnp.clip(first_ref[slot], 0, OWN - 1)
        b = second_ref[slot] + 2
        left = turned[a, mine, :]
        shift_ref[slot] = count * jnp.dot(
            left[:, :shards], dev[b], precision=lax.Precision.HIGHEST, preferred_element_type=F32
        )
        scale_ref[slot] = left[:, shards : shards + 1] * inv[pl.ds(b, 1), :] * (1.0 / total**0.5)


def factors(count, first, second, me, *stats):
    vmem = pl.BlockSpec(memory_space=VMEM)
    smem = pl.BlockSpec(memory_space=SMEM)
    return pl.pallas_call(
        functools.partial(factors_kernel, count),
        in_specs=[smem] * 3 + [vmem] * 3,
        out_specs=[vmem] * 2,
        out_shape=[jax.ShapeDtypeStruct((SLOTS, ROWS, BLK), F32)] * 2,
        scratch_shapes=[
            VMEM((OWN, BLK, 128), F32),
            VMEM((8, SHARDS, BLK), F32),
            VMEM((8, BLK), F32),
        ],
        compiler_params=pltpu.CompilerParams(vmem_limit_bytes=8 << 20),
        cost_estimate=pl.CostEstimate(flops=1 << 26, bytes_accessed=2 << 20, transcendentals=2048),
        name="factors",
    )(first, second, me, *stats)


def finish_kernel(slot_ref, main_ref, home_ref, shift_ref, scale_ref, out_ref, all_ref):
    all_ref[:MADE] = (main_ref[...] + shift_ref[:MADE]) * scale_ref[:MADE]
    all_ref[HOME] = (home_ref[...] + shift_ref[HOME]) * scale_ref[HOME]
    for p in range(PAIRS):
        out_ref[:, p, :] = all_ref[slot_ref[p]]


def finish(slot, main, home, shift, scale):
    vmem = pl.BlockSpec(memory_space=VMEM)
    return pl.pallas_call(
        finish_kernel,
        in_specs=[pl.BlockSpec(memory_space=SMEM)] + [vmem] * 4,
        out_specs=vmem,
        out_shape=jax.ShapeDtypeStruct((ROWS, PAIRS, BLK), F32),
        scratch_shapes=[VMEM((SLOTS, ROWS, BLK), F32)],
        compiler_params=pltpu.CompilerParams(vmem_limit_bytes=8 << 20),
        cost_estimate=pl.CostEstimate(flops=1 << 18, bytes_accessed=1 << 20, transcendentals=0),
        name="finish",
    )(slot, main, home, shift, scale)


def on_device(features, pairs):
    shots = features.shape[1]
    owners = lax.axis_size("det")
    owner = lax.axis_index("det").astype(jnp.int32)
    core = lax.rem(owner, 2)
    place = jnp.stack([owner * OWN, core])
    me = lax.axis_index("shot").astype(jnp.int32).reshape(1)

    def swap(x, start):
        ends = [(i, i + 1) for i in range(start, owners - 1, 2)]
        return lax.ppermute(x, "det", ends + [(b, a) for a, b in ends])

    to_a = border(3 * core, 1, features, "border_for_a")
    later, to_a = lax.optimization_barrier((2 - 2 * core, to_a))
    from_a = swap(to_a, 1)
    from_b = swap(border(later, 2, features, "border_for_b"), 0)
    tiles, parts, stats, first, second, slot, left, right = early(pairs, place, features)
    parts = split(6, from_a, parts)
    tiles, _ = near(left, right, from_b, parts, tiles)
    main = lax.psum_scatter(
        tiles.reshape(SHARDS * MADE * ROWS, BLK), "shot", scatter_dimension=0, tiled=True
    ).reshape(MADE, ROWS, BLK)

    stats, tiles = lax.optimization_barrier((stats, tiles))
    stats = lax.all_gather(stats.reshape(2 * OWN, BLK), "shot").reshape(-1, 2, OWN, BLK)
    up = [(i, i + 1) for i in range(owners - 1)]
    below = lax.ppermute(stats[:, :, 2:], "det", up)
    above = lax.ppermute(stats[:, :, :2], "det", [(b, a) for a, b in up])
    shift, scale = factors(float(shots), first, second, me, stats, below, above)
    return finish(slot, main, swap(main[15], 1), shift, scale)


def solution(mesh):
    in_specs = (P("det", "shot"), P("det", None))
    out_specs = P("shot", "det", None)
    return jax.shard_map(on_device, mesh=mesh, in_specs=in_specs, out_specs=out_specs, check_vma=False)
```

```python
import functools

import jax
import jax.numpy as jnp
from jax import lax
from jax.experimental import pallas as pl
from jax.experimental.pallas import tpu as pltpu
from jax.sharding import PartitionSpec as P

BLK = 256
OWN = 4
EARLY = 10
MADE = 16
PAIRS = 16
HOME = 16
SLOTS = 17
PLACES = 7
EARLY_GROUPS = (4, 3, 3)
NEAR_GROUPS = (3, 3)
SPLIT_COST = 1 << 34
SHARDS = 16
ROWS = BLK // SHARDS
F32 = jnp.float32
BF16 = jnp.bfloat16
SMEM = pltpu.SMEM
VMEM = pltpu.VMEM


def split_block(x, parts_ref, place, stats_ref, row):
    count = x.shape[1]
    mean = jnp.sum(x, axis=1, keepdims=True) * (1.0 / count)
    centered = x - mean
    hi = centered.astype(BF16)
    at = 2 * BLK * place
    parts_ref[at : at + BLK, :] = hi
    parts_ref[at + BLK : at + 2 * BLK, :] = (centered - hi.astype(F32)).astype(BF16)
    if stats_ref is None:
        return
    squares = jnp.sum(centered * centered, axis=1, keepdims=True)
    lane = lax.broadcasted_iota(jnp.int32, (BLK, 128), 1)
    both = jnp.where(lane < 8, jnp.broadcast_to(mean, (BLK, 128)), jnp.broadcast_to(squares, (BLK, 128)))
    flat = jnp.transpose(both)
    stats_ref[0, pl.ds(row, 1), :] = flat[0:1, :]
    stats_ref[1, pl.ds(row, 1), :] = flat[8:9, :]


def product(parts_ref, a, b):
    dot = functools.partial(
        lax.dot_general, dimension_numbers=(((1,), (1,)), ((), ())), preferred_element_type=F32
    )
    at = pl.multiple_of(a * (2 * BLK), 2 * BLK)
    by = pl.multiple_of(b * (2 * BLK), 2 * BLK)
    both = dot(parts_ref[pl.ds(at, 2 * BLK), :], parts_ref[pl.ds(by, BLK), :])
    rest = dot(parts_ref[pl.ds(at, BLK), :], parts_ref[pl.ds(by + BLK, BLK), :])
    return both[:BLK] + (both[BLK:] + rest)


def border_kernel(start_ref, x_ref, out_ref, held, in_sems, out_sems):
    rows = held.shape[1]
    loads, stores = [], []
    for k in range(held.shape[0]):
        here = pl.ds(pl.multiple_of(start_ref[0] * BLK + k * rows, rows), rows)
        loads.append(pltpu.make_async_copy(x_ref.at[here, :], held.at[k], in_sems.at[k]))
        stores.append(pltpu.make_async_copy(held.at[k], out_ref.at[pl.ds(k * rows, rows), :], out_sems.at[k]))
        loads[k].start()
    for load, store in zip(loads, stores):
        load.wait()
        store.start()
    for store in stores:
        store.wait()


def border(start, blocks, features, name):
    shots = features.shape[1]
    pieces = 4
    return pl.pallas_call(
        border_kernel,
        in_specs=[pl.BlockSpec(memory_space=SMEM), pl.BlockSpec(memory_space=pl.ANY)],
        out_specs=pl.BlockSpec(memory_space=pl.ANY),
        out_shape=pltpu.HBM((blocks * BLK, shots), F32),
        scratch_shapes=[
            VMEM((pieces, blocks * BLK // pieces, shots), F32),
            pltpu.SemaphoreType.DMA((pieces,)),
            pltpu.SemaphoreType.DMA((pieces,)),
        ],
        compiler_params=pltpu.CompilerParams(vmem_limit_bytes=8 << 20),
        cost_estimate=pl.CostEstimate(flops=0, bytes_accessed=blocks << 21, transcendentals=0),
        name=name,
    )(start.reshape(1), pltpu.with_memory_space_constraint(features, pltpu.HBM))


def assign(pairs_ref, base, core, first_ref, second_ref, slot_ref, left_ref, right_ref):
    def kind_of(p):
        second = pairs_ref[p, 1] - base
        own = jnp.logical_and(second >= 0, second < OWN)
        near = jnp.logical_and(second >= -1, second <= OWN)
        with_a = (second < 0) == (core == 0)
        return jnp.where(own, 0, jnp.where(with_a, jnp.where(near, 2, 3), 1))

    first_ref[HOME] = 0
    second_ref[HOME] = 0
    first_ref[15] = jnp.where(core == 0, -1, OWN)
    second_ref[15] = jnp.where(core == 0, 1, 2)
    kinds = [kind_of(p) for p in range(PAIRS)]
    n_in, n_with_b = (sum((kind == k).astype(jnp.int32) for kind in kinds) for k in range(2))
    places = [jnp.int32(0), jnp.int32(EARLY), n_in + n_with_b]
    for p, kind in enumerate(kinds):
        own = places[0] + jnp.where(places[0] >= EARLY, n_with_b, 0)
        place = jnp.where(kind == 0, own, jnp.where(kind == 1, places[1], places[2]))
        slot = jnp.where(kind == 3, HOME, place)
        places = [place + (kind == k).astype(jnp.int32) for k, place in enumerate(places)]
        slot_ref[p] = slot
        first_ref[slot] = pairs_ref[p, 0] - base
        second_ref[slot] = pairs_ref[p, 1] - base

    def place_of(block):
        with_a = (block < 0) == (core == 0)
        beside = jnp.where(with_a, 6, jnp.where(block < 0, block + 6, block))
        return jnp.where(jnp.logical_and(block >= 0, block < OWN), block, beside)

    for slot in range(MADE):
        left_ref[slot] = place_of(first_ref[slot])
        right_ref[slot] = place_of(second_ref[slot])


def fill(start, counts, parts_ref, left_ref, right_ref, tiles_ref, buffers, sems):
    def copy(k):
        return pltpu.make_async_copy(buffers.at[k], tiles_ref.at[:, start + k], sems.at[k])

    done = 0
    for count in counts:
        group = range(done, done + count)
        tiles = [product(parts_ref, left_ref[start + k], right_ref[start + k]) for k in group]
        for k, tile in zip(group, tiles):
            buffers[k] = tile.reshape(SHARDS, ROWS, BLK)
            copy(k).start()
        done += count
    for k in range(done):
        copy(k).wait()


def early_kernel(
    pairs_ref, place_ref, x_ref, tiles_ref, parts_ref, stats_ref, first_ref, second_ref, slot_ref, left_ref, right_ref,
    x_vmem, buffers, in_sems, out_sems,
):
    loads = [
        pltpu.make_async_copy(x_ref.at[pl.ds(k * BLK, BLK), :], x_vmem.at[k], in_sems.at[k]) for k in range(OWN)
    ]
    for load in loads:
        load.start()
    assign(pairs_ref, place_ref[0], place_ref[1], first_ref, second_ref, slot_ref, left_ref, right_ref)
    for k, load in enumerate(loads):
        load.wait()
        split_block(x_vmem[k], parts_ref, k, stats_ref, k)
    fill(0, EARLY_GROUPS, parts_ref, left_ref, right_ref, tiles_ref, buffers, out_sems)


def early(pairs, place, features):
    shots = features.shape[1]
    smem, vmem, anywhere = (pl.BlockSpec(memory_space=space) for space in (SMEM, VMEM, pl.ANY))
    numbers = jax.ShapeDtypeStruct((SLOTS,), jnp.int32)
    return pl.pallas_call(
        early_kernel,
        in_specs=[smem, smem, anywhere],
        out_specs=[anywhere, vmem, vmem] + [smem] * 5,
        out_shape=[
            pltpu.HBM((SHARDS, MADE, ROWS, BLK), F32),
            jax.ShapeDtypeStruct((PLACES * 2 * BLK, shots), BF16),
            jax.ShapeDtypeStruct((2, OWN, BLK), F32),
            numbers,
            numbers,
            jax.ShapeDtypeStruct((PAIRS,), jnp.int32),
            numbers,
            numbers,
        ],
        scratch_shapes=[
            VMEM((OWN, BLK, shots), F32),
            VMEM((EARLY, SHARDS, ROWS, BLK), F32),
            pltpu.SemaphoreType.DMA((OWN,)),
            pltpu.SemaphoreType.DMA((EARLY,)),
        ],
        compiler_params=pltpu.CompilerParams(vmem_limit_bytes=24 << 20),
        cost_estimate=pl.CostEstimate(flops=6 * EARLY * BLK * BLK * shots, bytes_accessed=12 << 20, transcendentals=0),
        name="early_tiles",
    )(pairs, place, pltpu.with_memory_space_constraint(features, pltpu.HBM))


def split_kernel(place, halo_ref, _, parts_ref):
    split_block(halo_ref[...], parts_ref, place, None, None)


def split(place, halo, parts):
    vmem = pl.BlockSpec(memory_space=VMEM)
    return pl.pallas_call(
        functools.partial(split_kernel, place),
        in_specs=[vmem, vmem],
        out_specs=vmem,
        out_shape=jax.ShapeDtypeStruct(parts.shape, BF16),
        input_output_aliases={1: 0},
        compiler_params=pltpu.CompilerParams(vmem_limit_bytes=8 << 20),
        cost_estimate=pl.CostEstimate(flops=SPLIT_COST, bytes_accessed=1 << 20, transcendentals=0),
        name="split_a",
    )(halo, parts)


def near_kernel(left_ref, right_ref, halo_ref, _, __, tiles_ref, parts_ref, buffers, sems):
    for k in range(2):
        split_block(halo_ref[k * BLK : (k + 1) * BLK, :], parts_ref, OWN + k, None, None)
    fill(EARLY, NEAR_GROUPS, parts_ref, left_ref, right_ref, tiles_ref, buffers, sems)


def near(left, right, halo, parts, tiles):
    smem, vmem, anywhere = (pl.BlockSpec(memory_space=space) for space in (SMEM, VMEM, pl.ANY))
    count = MADE - EARLY
    return pl.pallas_call(
        near_kernel,
        in_specs=[smem, smem, vmem, vmem, anywhere],
        out_specs=[anywhere, vmem],
        out_shape=[pltpu.HBM(tiles.shape, F32), jax.ShapeDtypeStruct(parts.shape, BF16)],
        scratch_shapes=[VMEM((count, SHARDS, ROWS, BLK), F32), pltpu.SemaphoreType.DMA((count,))],
        input_output_aliases={3: 1, 4: 0},
        compiler_params=pltpu.CompilerParams(vmem_limit_bytes=16 << 20),
        cost_estimate=pl.CostEstimate(
            flops=6 * count * BLK * BLK * halo.shape[1], bytes_accessed=5 << 20, transcendentals=0
        ),
        name="near_tiles",
    )(left, right, halo, parts, tiles)


def factors_kernel(
    count, first_ref, second_ref, me_ref, own_ref, below_ref, above_ref, main_ref, done_ref, shift_ref, scale_ref,
    turned, dev, inv, tiles, sem,
):
    fetch = pltpu.make_async_copy(main_ref, tiles, sem)
    fetch.start()
    shards = own_ref.shape[0]
    total = shards * count
    stats = jnp.concatenate([below_ref[...], own_ref[...], above_ref[...]], axis=2)
    means, squares = stats[:, 0], stats[:, 1]
    mean = jnp.sum(means, axis=0) * (1.0 / shards)
    away = means - mean[None]
    squares = jnp.sum(squares, axis=0) + count * jnp.sum(away * away, axis=0)
    inverse = lax.rsqrt(squares * (1.0 / total) + 1e-06)
    inv[...] = inverse
    for block in range(8):
        dev[block] = away[:, block, :]
    for block in range(OWN):
        column = jnp.concatenate(
            [away[:, 2 + block, :], jnp.broadcast_to(inverse[2 + block : 3 + block, :], (128 - shards, BLK))], axis=0
        )
        turned[block] = jnp.transpose(column)
    mine = pl.ds(pl.multiple_of(me_ref[0] * ROWS, ROWS), ROWS)
    for slot in range(SLOTS):
        a = jnp.clip(first_ref[slot], 0, OWN - 1)
        b = second_ref[slot] + 2
        left = turned[a, mine, :]
        shift = count * jnp.dot(
            left[:, :shards], dev[b], precision=lax.Precision.HIGHEST, preferred_element_type=F32
        )
        scale = left[:, shards : shards + 1] * inv[pl.ds(b, 1), :] * (1.0 / total**0.5)
        if slot == 0:
            fetch.wait()
        if slot == HOME:
            shift_ref[...] = shift
            scale_ref[...] = scale
        else:
            done_ref[slot] = (tiles[slot] + shift) * scale


def factors(count, first, second, me, own, below, above, main):
    vmem = pl.BlockSpec(memory_space=VMEM)
    smem = pl.BlockSpec(memory_space=SMEM)
    return pl.pallas_call(
        functools.partial(factors_kernel, count),
        in_specs=[smem] * 3 + [vmem] * 3 + [pl.BlockSpec(memory_space=pl.ANY)],
        out_specs=[vmem] * 3,
        out_shape=[jax.ShapeDtypeStruct((MADE, ROWS, BLK), F32)] + [jax.ShapeDtypeStruct((ROWS, BLK), F32)] * 2,
        scratch_shapes=[
            VMEM((OWN, BLK, 128), F32),
            VMEM((8, SHARDS, BLK), F32),
            VMEM((8, BLK), F32),
            VMEM((MADE, ROWS, BLK), F32),
            pltpu.SemaphoreType.DMA,
        ],
        compiler_params=pltpu.CompilerParams(vmem_limit_bytes=8 << 20),
        cost_estimate=pl.CostEstimate(flops=1 << 26, bytes_accessed=2 << 20, transcendentals=2048),
        name="factors",
    )(first, second, me, own, below, above, pltpu.with_memory_space_constraint(main, pltpu.HBM))


def finish_kernel(slot_ref, done_ref, home_ref, shift_ref, scale_ref, out_ref, home):
    home[...] = (home_ref[...] + shift_ref[...]) * scale_ref[...]
    for p in range(PAIRS):
        slot = slot_ref[p]
        made = done_ref[jnp.minimum(slot, MADE - 1)]
        out_ref[:, p, :] = jnp.where(slot == HOME, home[...], made)


def finish(slot, done, home, shift, scale):
    vmem = pl.BlockSpec(memory_space=VMEM)
    return pl.pallas_call(
        finish_kernel,
        in_specs=[pl.BlockSpec(memory_space=SMEM)] + [vmem] * 4,
        out_specs=vmem,
        out_shape=jax.ShapeDtypeStruct((ROWS, PAIRS, BLK), F32),
        scratch_shapes=[VMEM((ROWS, BLK), F32)],
        compiler_params=pltpu.CompilerParams(vmem_limit_bytes=8 << 20),
        cost_estimate=pl.CostEstimate(flops=1 << 18, bytes_accessed=1 << 20, transcendentals=0),
        name="finish",
    )(slot, done, home, shift, scale)


def on_device(features, pairs):
    shots = features.shape[1]
    owners = lax.axis_size("det")
    owner = lax.axis_index("det").astype(jnp.int32)
    core = lax.rem(owner, 2)
    place = jnp.stack([owner * OWN, core])
    me = lax.axis_index("shot").astype(jnp.int32).reshape(1)

    def swap(x, start):
        ends = [(i, i + 1) for i in range(start, owners - 1, 2)]
        return lax.ppermute(x, "det", ends + [(b, a) for a, b in ends])

    to_a = border(3 * core, 1, features, "border_for_a")
    later, to_a = lax.optimization_barrier((2 - 2 * core, to_a))
    from_a = swap(to_a, 1)
    from_b = swap(border(later, 2, features, "border_for_b"), 0)
    tiles, parts, stats, first, second, slot, left, right = early(pairs, place, features)
    parts = split(6, from_a, parts)
    tiles, _ = near(left, right, from_b, parts, tiles)
    main = lax.psum_scatter(
        tiles.reshape(SHARDS * MADE * ROWS, BLK), "shot", scatter_dimension=0, tiled=True
    ).reshape(MADE, ROWS, BLK)

    stats, tiles = lax.optimization_barrier((stats, tiles))
    stats = lax.all_gather(stats.reshape(2 * OWN, BLK), "shot").reshape(-1, 2, OWN, BLK)
    up = [(i, i + 1) for i in range(owners - 1)]
    below = lax.ppermute(stats[:, :, 2:], "det", up)
    above = lax.ppermute(stats[:, :, :2], "det", [(b, a) for a, b in up])
    home = swap(main[15], 1)
    done, shift, scale = factors(float(shots), first, second, me, stats, below, above, main)
    return finish(slot, done, home, shift, scale)


def solution(mesh):
    in_specs = (P("det", "shot"), P("det", None))
    out_specs = P("shot", "det", None)
    return jax.shard_map(on_device, mesh=mesh, in_specs=in_specs, out_specs=out_specs, check_vma=False)
```

```python
import functools

import jax
import jax.numpy as jnp
from jax import lax
from jax.experimental import pallas as pl
from jax.experimental.pallas import tpu as pltpu
from jax.sharding import PartitionSpec as P

BLK = 256
OWN = 4
EARLY = 10
MADE = 16
PAIRS = 16
HOME = 16
SLOTS = 17
PLACES = 7
EARLY_GROUPS = (4, 3, 3)
NEAR_GROUPS = (3, 3)
SPLIT_COST = 1 << 34
SHARDS = 16
ROWS = BLK // SHARDS
F32 = jnp.float32
BF16 = jnp.bfloat16
SMEM = pltpu.SMEM
VMEM = pltpu.VMEM


def split_block(x, parts_ref, place, stats_ref, row):
    count = x.shape[1]
    mean = jnp.sum(x, axis=1, keepdims=True) * (1.0 / count)
    centered = x - mean
    hi = centered.astype(BF16)
    at = 2 * BLK * place
    parts_ref[at : at + BLK, :] = hi
    parts_ref[at + BLK : at + 2 * BLK, :] = (centered - hi.astype(F32)).astype(BF16)
    if stats_ref is None:
        return
    squares = jnp.sum(centered * centered, axis=1, keepdims=True)
    lane = lax.broadcasted_iota(jnp.int32, (BLK, 128), 1)
    both = jnp.where(lane < 8, jnp.broadcast_to(mean, (BLK, 128)), jnp.broadcast_to(squares, (BLK, 128)))
    flat = jnp.transpose(both)
    stats_ref[0, pl.ds(row, 1), :] = flat[0:1, :]
    stats_ref[1, pl.ds(row, 1), :] = flat[8:9, :]


def product(parts_ref, a, b):
    dot = functools.partial(
        lax.dot_general, dimension_numbers=(((1,), (1,)), ((), ())), preferred_element_type=F32
    )
    at = pl.multiple_of(a * (2 * BLK), 2 * BLK)
    by = pl.multiple_of(b * (2 * BLK), 2 * BLK)
    both = dot(parts_ref[pl.ds(at, 2 * BLK), :], parts_ref[pl.ds(by, BLK), :])
    rest = dot(parts_ref[pl.ds(at, BLK), :], parts_ref[pl.ds(by + BLK, BLK), :])
    return both[:BLK] + (both[BLK:] + rest)


def border_kernel(start_ref, x_ref, out_ref, held, in_sems, out_sems):
    rows = held.shape[1]
    loads, stores = [], []
    for k in range(held.shape[0]):
        here = pl.ds(pl.multiple_of(start_ref[0] * BLK + k * rows, rows), rows)
        loads.append(pltpu.make_async_copy(x_ref.at[here, :], held.at[k], in_sems.at[k]))
        stores.append(pltpu.make_async_copy(held.at[k], out_ref.at[pl.ds(k * rows, rows), :], out_sems.at[k]))
        loads[k].start()
    for load, store in zip(loads, stores):
        load.wait()
        store.start()
    for store in stores:
        store.wait()


def border_held_kernel(start_ref, x_ref, out_ref, sem):
    copy = pltpu.make_async_copy(x_ref.at[pl.ds(start_ref[0] * BLK, BLK), :], out_ref, sem)
    copy.start()
    copy.wait()


def border_held(start, features):
    shots = features.shape[1]
    return pl.pallas_call(
        border_held_kernel,
        in_specs=[pl.BlockSpec(memory_space=SMEM), pl.BlockSpec(memory_space=pl.ANY)],
        out_specs=pl.BlockSpec(memory_space=VMEM),
        out_shape=jax.ShapeDtypeStruct((BLK, shots), F32),
        scratch_shapes=[pltpu.SemaphoreType.DMA],
        compiler_params=pltpu.CompilerParams(vmem_limit_bytes=8 << 20),
        cost_estimate=pl.CostEstimate(flops=0, bytes_accessed=2 << 20, transcendentals=0),
        name="border_for_a",
    )(start.reshape(1), pltpu.with_memory_space_constraint(features, pltpu.HBM))


def border(start, blocks, features, name):
    shots = features.shape[1]
    pieces = 4
    return pl.pallas_call(
        border_kernel,
        in_specs=[pl.BlockSpec(memory_space=SMEM), pl.BlockSpec(memory_space=pl.ANY)],
        out_specs=pl.BlockSpec(memory_space=pl.ANY),
        out_shape=pltpu.HBM((blocks * BLK, shots), F32),
        scratch_shapes=[
            VMEM((pieces, blocks * BLK // pieces, shots), F32),
            pltpu.SemaphoreType.DMA((pieces,)),
            pltpu.SemaphoreType.DMA((pieces,)),
        ],
        compiler_params=pltpu.CompilerParams(vmem_limit_bytes=8 << 20),
        cost_estimate=pl.CostEstimate(flops=0, bytes_accessed=blocks << 21, transcendentals=0),
        name=name,
    )(start.reshape(1), pltpu.with_memory_space_constraint(features, pltpu.HBM))


def assign(pairs_ref, base, core, first_ref, second_ref, slot_ref, left_ref, right_ref):
    def kind_of(p):
        second = pairs_ref[p, 1] - base
        own = jnp.logical_and(second >= 0, second < OWN)
        near = jnp.logical_and(second >= -1, second <= OWN)
        with_a = (second < 0) == (core == 0)
        return jnp.where(own, 0, jnp.where(with_a, jnp.where(near, 2, 3), 1))

    first_ref[HOME] = 0
    second_ref[HOME] = 0
    first_ref[15] = jnp.where(core == 0, -1, OWN)
    second_ref[15] = jnp.where(core == 0, 1, 2)
    kinds = [kind_of(p) for p in range(PAIRS)]
    n_in, n_with_b = (sum((kind == k).astype(jnp.int32) for kind in kinds) for k in range(2))
    places = [jnp.int32(0), jnp.int32(EARLY), n_in + n_with_b]
    for p, kind in enumerate(kinds):
        own = places[0] + jnp.where(places[0] >= EARLY, n_with_b, 0)
        place = jnp.where(kind == 0, own, jnp.where(kind == 1, places[1], places[2]))
        slot = jnp.where(kind == 3, HOME, place)
        places = [place + (kind == k).astype(jnp.int32) for k, place in enumerate(places)]
        slot_ref[p] = slot
        first_ref[slot] = pairs_ref[p, 0] - base
        second_ref[slot] = pairs_ref[p, 1] - base

    def place_of(block):
        with_a = (block < 0) == (core == 0)
        beside = jnp.where(with_a, 6, jnp.where(block < 0, block + 6, block))
        return jnp.where(jnp.logical_and(block >= 0, block < OWN), block, beside)

    for slot in range(MADE):
        left_ref[slot] = place_of(first_ref[slot])
        right_ref[slot] = place_of(second_ref[slot])


def fill(start, counts, parts_ref, left_ref, right_ref, tiles_ref, buffers, sems):
    def copy(k):
        return pltpu.make_async_copy(buffers.at[k], tiles_ref.at[:, start + k], sems.at[k])

    done = 0
    for count in counts:
        group = range(done, done + count)
        tiles = [product(parts_ref, left_ref[start + k], right_ref[start + k]) for k in group]
        for k, tile in zip(group, tiles):
            buffers[k] = tile.reshape(SHARDS, ROWS, BLK)
            copy(k).start()
        done += count
    for k in range(done):
        copy(k).wait()


def early_kernel(
    pairs_ref, place_ref, x_ref, tiles_ref, parts_ref, stats_ref, first_ref, second_ref, slot_ref, left_ref, right_ref,
    x_vmem, buffers, in_sems, out_sems,
):
    loads = [
        pltpu.make_async_copy(x_ref.at[pl.ds(k * BLK, BLK), :], x_vmem.at[k], in_sems.at[k]) for k in range(OWN)
    ]
    for load in loads:
        load.start()
    assign(pairs_ref, place_ref[0], place_ref[1], first_ref, second_ref, slot_ref, left_ref, right_ref)
    for k, load in enumerate(loads):
        load.wait()
        split_block(x_vmem[k], parts_ref, k, stats_ref, k)
    fill(0, EARLY_GROUPS, parts_ref, left_ref, right_ref, tiles_ref, buffers, out_sems)


def early(pairs, place, features):
    shots = features.shape[1]
    smem, vmem, anywhere = (pl.BlockSpec(memory_space=space) for space in (SMEM, VMEM, pl.ANY))
    numbers = jax.ShapeDtypeStruct((SLOTS,), jnp.int32)
    return pl.pallas_call(
        early_kernel,
        in_specs=[smem, smem, anywhere],
        out_specs=[anywhere, vmem, vmem] + [smem] * 5,
        out_shape=[
            pltpu.HBM((SHARDS, MADE, ROWS, BLK), F32),
            jax.ShapeDtypeStruct((PLACES * 2 * BLK, shots), BF16),
            jax.ShapeDtypeStruct((2, OWN, BLK), F32),
            numbers,
            numbers,
            jax.ShapeDtypeStruct((PAIRS,), jnp.int32),
            numbers,
            numbers,
        ],
        scratch_shapes=[
            VMEM((OWN, BLK, shots), F32),
            VMEM((EARLY, SHARDS, ROWS, BLK), F32),
            pltpu.SemaphoreType.DMA((OWN,)),
            pltpu.SemaphoreType.DMA((EARLY,)),
        ],
        compiler_params=pltpu.CompilerParams(vmem_limit_bytes=24 << 20),
        cost_estimate=pl.CostEstimate(flops=6 * EARLY * BLK * BLK * shots, bytes_accessed=12 << 20, transcendentals=0),
        name="early_tiles",
    )(pairs, place, pltpu.with_memory_space_constraint(features, pltpu.HBM))


def split_kernel(place, halo_ref, _, parts_ref):
    split_block(halo_ref[...], parts_ref, place, None, None)


def split(place, halo, parts):
    vmem = pl.BlockSpec(memory_space=VMEM)
    return pl.pallas_call(
        functools.partial(split_kernel, place),
        in_specs=[vmem, vmem],
        out_specs=vmem,
        out_shape=jax.ShapeDtypeStruct(parts.shape, BF16),
        input_output_aliases={1: 0},
        compiler_params=pltpu.CompilerParams(vmem_limit_bytes=8 << 20),
        cost_estimate=pl.CostEstimate(flops=SPLIT_COST, bytes_accessed=1 << 20, transcendentals=0),
        name="split_a",
    )(halo, parts)


def near_kernel(left_ref, right_ref, halo_ref, before_ref, _, tiles_ref, parts_ref, buffers, sems):

    def copy(k):
        return pltpu.make_async_copy(buffers.at[k], tiles_ref.at[:, EARLY + k], sems.at[k])

    with_b = MADE - EARLY - 3
    ahead = [product(before_ref, left_ref[EARLY + k], right_ref[EARLY + k]) for k in range(with_b, MADE - EARLY)]
    for k, tile in enumerate(ahead):
        buffers[with_b + k] = tile.reshape(SHARDS, ROWS, BLK)
        copy(with_b + k).start()
    for k in range(2):
        split_block(halo_ref[k * BLK : (k + 1) * BLK, :], parts_ref, OWN + k, None, None)
    fill(EARLY, (with_b,), parts_ref, left_ref, right_ref, tiles_ref, buffers, sems)
    for k in range(with_b, MADE - EARLY):
        copy(k).wait()


def near(left, right, halo, parts, tiles):
    smem, vmem, anywhere = (pl.BlockSpec(memory_space=space) for space in (SMEM, VMEM, pl.ANY))
    count = MADE - EARLY
    return pl.pallas_call(
        near_kernel,
        in_specs=[smem, smem, vmem, vmem, anywhere],
        out_specs=[anywhere, vmem],
        out_shape=[pltpu.HBM(tiles.shape, F32), jax.ShapeDtypeStruct(parts.shape, BF16)],
        scratch_shapes=[VMEM((count, SHARDS, ROWS, BLK), F32), pltpu.SemaphoreType.DMA((count,))],
        input_output_aliases={3: 1, 4: 0},
        compiler_params=pltpu.CompilerParams(vmem_limit_bytes=16 << 20),
        cost_estimate=pl.CostEstimate(
            flops=6 * count * BLK * BLK * halo.shape[1], bytes_accessed=5 << 20, transcendentals=0
        ),
        name="near_tiles",
    )(left, right, halo, parts, tiles)


def factors_kernel(
    count, first_ref, second_ref, me_ref, own_ref, below_ref, above_ref, main_ref, done_ref, shift_ref, scale_ref,
    turned, dev, inv, tiles, sem,
):
    fetch = pltpu.make_async_copy(main_ref, tiles, sem)
    fetch.start()
    shards = own_ref.shape[0]
    total = shards * count
    stats = jnp.concatenate([below_ref[...], own_ref[...], above_ref[...]], axis=2)
    means, squares = stats[:, 0], stats[:, 1]
    mean = jnp.sum(means, axis=0) * (1.0 / shards)
    away = means - mean[None]
    squares = jnp.sum(squares, axis=0) + count * jnp.sum(away * away, axis=0)
    inverse = lax.rsqrt(squares * (1.0 / total) + 1e-06)
    inv[...] = inverse
    for block in range(8):
        dev[block] = away[:, block, :]
    for block in range(OWN):
        column = jnp.concatenate(
            [away[:, 2 + block, :], jnp.broadcast_to(inverse[2 + block : 3 + block, :], (128 - shards, BLK))], axis=0
        )
        turned[block] = jnp.transpose(column)
    mine = pl.ds(pl.multiple_of(me_ref[0] * ROWS, ROWS), ROWS)
    for slot in range(SLOTS):
        a = jnp.clip(first_ref[slot], 0, OWN - 1)
        b = second_ref[slot] + 2
        left = turned[a, mine, :]
        shift = count * jnp.dot(
            left[:, :shards], dev[b], precision=lax.Precision.HIGHEST, preferred_element_type=F32
        )
        scale = left[:, shards : shards + 1] * inv[pl.ds(b, 1), :] * (1.0 / total**0.5)
        if slot == 0:
            fetch.wait()
        if slot == HOME:
            shift_ref[...] = shift
            scale_ref[...] = scale
        else:
            done_ref[slot] = (tiles[slot] + shift) * scale


def factors(count, first, second, me, own, below, above, main):
    vmem = pl.BlockSpec(memory_space=VMEM)
    smem = pl.BlockSpec(memory_space=SMEM)
    return pl.pallas_call(
        functools.partial(factors_kernel, count),
        in_specs=[smem] * 3 + [vmem] * 3 + [pl.BlockSpec(memory_space=pl.ANY)],
        out_specs=[vmem] * 3,
        out_shape=[jax.ShapeDtypeStruct((MADE, ROWS, BLK), F32)] + [jax.ShapeDtypeStruct((ROWS, BLK), F32)] * 2,
        scratch_shapes=[
            VMEM((OWN, BLK, 128), F32),
            VMEM((8, SHARDS, BLK), F32),
            VMEM((8, BLK), F32),
            VMEM((MADE, ROWS, BLK), F32),
            pltpu.SemaphoreType.DMA,
        ],
        compiler_params=pltpu.CompilerParams(vmem_limit_bytes=8 << 20),
        cost_estimate=pl.CostEstimate(flops=1 << 26, bytes_accessed=2 << 20, transcendentals=2048),
        name="factors",
    )(first, second, me, own, below, above, pltpu.with_memory_space_constraint(main, pltpu.HBM))


def finish_kernel(slot_ref, done_ref, home_ref, shift_ref, scale_ref, out_ref, home):
    home[...] = (home_ref[...] + shift_ref[...]) * scale_ref[...]
    for p in range(PAIRS):
        slot = slot_ref[p]
        made = done_ref[jnp.minimum(slot, MADE - 1)]
        out_ref[:, p, :] = jnp.where(slot == HOME, home[...], made)


def finish(slot, done, home, shift, scale):
    vmem = pl.BlockSpec(memory_space=VMEM)
    return pl.pallas_call(
        finish_kernel,
        in_specs=[pl.BlockSpec(memory_space=SMEM)] + [vmem] * 4,
        out_specs=vmem,
        out_shape=jax.ShapeDtypeStruct((ROWS, PAIRS, BLK), F32),
        scratch_shapes=[VMEM((ROWS, BLK), F32)],
        compiler_params=pltpu.CompilerParams(vmem_limit_bytes=8 << 20),
        cost_estimate=pl.CostEstimate(flops=1 << 18, bytes_accessed=1 << 20, transcendentals=0),
        name="finish",
    )(slot, done, home, shift, scale)


def on_device(features, pairs):
    shots = features.shape[1]
    owners = lax.axis_size("det")
    owner = lax.axis_index("det").astype(jnp.int32)
    core = lax.rem(owner, 2)
    place = jnp.stack([owner * OWN, core])
    me = lax.axis_index("shot").astype(jnp.int32).reshape(1)

    def swap(x, start):
        ends = [(i, i + 1) for i in range(start, owners - 1, 2)]
        return lax.ppermute(x, "det", ends + [(b, a) for a, b in ends])

    to_a = border_held(3 * core, features)
    later, to_a = lax.optimization_barrier((2 - 2 * core, to_a))
    from_a = swap(to_a, 1)
    from_b = swap(border(later, 2, features, "border_for_b"), 0)
    tiles, parts, stats, first, second, slot, left, right = early(pairs, place, features)
    parts = split(6, from_a, parts)
    tiles, _ = near(left, right, from_b, parts, tiles)
    main = lax.psum_scatter(
        tiles.reshape(SHARDS * MADE * ROWS, BLK), "shot", scatter_dimension=0, tiled=True
    ).reshape(MADE, ROWS, BLK)

    stats, tiles = lax.optimization_barrier((stats, tiles))
    stats = lax.all_gather(stats.reshape(2 * OWN, BLK), "shot").reshape(-1, 2, OWN, BLK)
    up = [(i, i + 1) for i in range(owners - 1)]
    below = lax.ppermute(stats[:, :, 2:], "det", up)
    above = lax.ppermute(stats[:, :, :2], "det", [(b, a) for a, b in up])
    home = swap(main[15], 1)
    done, shift, scale = factors(float(shots), first, second, me, stats, below, above, main)
    return finish(slot, done, home, shift, scale)


def solution(mesh):
    in_specs = (P("det", "shot"), P("det", None))
    out_specs = P("shot", "det", None)
    return jax.shard_map(on_device, mesh=mesh, in_specs=in_specs, out_specs=out_specs, check_vma=False)
```

```python
import functools

import jax
import jax.numpy as jnp
from jax import lax
from jax.experimental import pallas as pl
from jax.experimental.pallas import tpu as pltpu
from jax.sharding import PartitionSpec as P

BLK = 256
OWN = 4
EARLY = 10
MADE = 16
PAIRS = 16
HOME = 16
SLOTS = 17
PLACES = 7
EARLY_GROUPS = (4, 3, 3)
NEAR_GROUPS = (3, 3)
SPLIT_COST = 1 << 34
SHARDS = 16
ROWS = BLK // SHARDS
F32 = jnp.float32
BF16 = jnp.bfloat16
SMEM = pltpu.SMEM
VMEM = pltpu.VMEM


def split_block(x, parts_ref, place, stats_ref, row):
    count = x.shape[1]
    mean = jnp.sum(x, axis=1, keepdims=True) * (1.0 / count)
    centered = x - mean
    hi = centered.astype(BF16)
    at = 2 * BLK * place
    parts_ref[at : at + BLK, :] = hi
    parts_ref[at + BLK : at + 2 * BLK, :] = (centered - hi.astype(F32)).astype(BF16)
    if stats_ref is None:
        return
    squares = jnp.sum(centered * centered, axis=1, keepdims=True)
    lane = lax.broadcasted_iota(jnp.int32, (BLK, 128), 1)
    both = jnp.where(lane < 8, jnp.broadcast_to(mean, (BLK, 128)), jnp.broadcast_to(squares, (BLK, 128)))
    flat = jnp.transpose(both)
    stats_ref[0, pl.ds(row, 1), :] = flat[0:1, :]
    stats_ref[1, pl.ds(row, 1), :] = flat[8:9, :]


def product(parts_ref, a, b):
    dot = functools.partial(
        lax.dot_general, dimension_numbers=(((1,), (1,)), ((), ())), preferred_element_type=F32
    )
    at = pl.multiple_of(a * (2 * BLK), 2 * BLK)
    by = pl.multiple_of(b * (2 * BLK), 2 * BLK)
    both = dot(parts_ref[pl.ds(at, 2 * BLK), :], parts_ref[pl.ds(by, BLK), :])
    rest = dot(parts_ref[pl.ds(at, BLK), :], parts_ref[pl.ds(by + BLK, BLK), :])
    return both[:BLK] + (both[BLK:] + rest)


def border_kernel(start_ref, x_ref, out_ref, held, in_sems, out_sems):
    rows = held.shape[1]
    loads, stores = [], []
    for k in range(held.shape[0]):
        here = pl.ds(pl.multiple_of(start_ref[0] * BLK + k * rows, rows), rows)
        loads.append(pltpu.make_async_copy(x_ref.at[here, :], held.at[k], in_sems.at[k]))
        stores.append(pltpu.make_async_copy(held.at[k], out_ref.at[pl.ds(k * rows, rows), :], out_sems.at[k]))
        loads[k].start()
    for load, store in zip(loads, stores):
        load.wait()
        store.start()
    for store in stores:
        store.wait()


def border(start, blocks, features, name):
    shots = features.shape[1]
    pieces = 4
    return pl.pallas_call(
        border_kernel,
        in_specs=[pl.BlockSpec(memory_space=SMEM), pl.BlockSpec(memory_space=pl.ANY)],
        out_specs=pl.BlockSpec(memory_space=pl.ANY),
        out_shape=pltpu.HBM((blocks * BLK, shots), F32),
        scratch_shapes=[
            VMEM((pieces, blocks * BLK // pieces, shots), F32),
            pltpu.SemaphoreType.DMA((pieces,)),
            pltpu.SemaphoreType.DMA((pieces,)),
        ],
        compiler_params=pltpu.CompilerParams(vmem_limit_bytes=8 << 20),
        cost_estimate=pl.CostEstimate(flops=0, bytes_accessed=blocks << 21, transcendentals=0),
        name=name,
    )(start.reshape(1), pltpu.with_memory_space_constraint(features, pltpu.HBM))


def assign(pairs_ref, base, core, first_ref, second_ref, slot_ref, left_ref, right_ref):
    def kind_of(p):
        second = pairs_ref[p, 1] - base
        own = jnp.logical_and(second >= 0, second < OWN)
        near = jnp.logical_and(second >= -1, second <= OWN)
        with_a = (second < 0) == (core == 0)
        return jnp.where(own, 0, jnp.where(with_a, jnp.where(near, 2, 3), 1))

    first_ref[HOME] = 0
    second_ref[HOME] = 0
    first_ref[15] = jnp.where(core == 0, -1, OWN)
    second_ref[15] = jnp.where(core == 0, 1, 2)
    kinds = [kind_of(p) for p in range(PAIRS)]
    n_in, n_with_b = (sum((kind == k).astype(jnp.int32) for kind in kinds) for k in range(2))
    places = [jnp.int32(0), jnp.int32(EARLY), n_in + n_with_b]
    for p, kind in enumerate(kinds):
        own = places[0] + jnp.where(places[0] >= EARLY, n_with_b, 0)
        place = jnp.where(kind == 0, own, jnp.where(kind == 1, places[1], places[2]))
        slot = jnp.where(kind == 3, HOME, place)
        places = [place + (kind == k).astype(jnp.int32) for k, place in enumerate(places)]
        slot_ref[p] = slot
        first_ref[slot] = pairs_ref[p, 0] - base
        second_ref[slot] = pairs_ref[p, 1] - base

    def place_of(block):
        with_a = (block < 0) == (core == 0)
        beside = jnp.where(with_a, 6, jnp.where(block < 0, block + 6, block))
        return jnp.where(jnp.logical_and(block >= 0, block < OWN), block, beside)

    for slot in range(MADE):
        left_ref[slot] = place_of(first_ref[slot])
        right_ref[slot] = place_of(second_ref[slot])


def fill(start, counts, parts_ref, left_ref, right_ref, tiles_ref, buffers, sems):
    def copy(k):
        return pltpu.make_async_copy(buffers.at[k], tiles_ref.at[:, start + k], sems.at[k])

    done = 0
    for count in counts:
        group = range(done, done + count)
        tiles = [product(parts_ref, left_ref[start + k], right_ref[start + k]) for k in group]
        for k, tile in zip(group, tiles):
            buffers[k] = tile.reshape(SHARDS, ROWS, BLK)
            copy(k).start()
        done += count
    for k in range(done):
        copy(k).wait()


def early_kernel(
    pairs_ref, place_ref, x_ref, tiles_ref, parts_ref, stats_ref, first_ref, second_ref, slot_ref, left_ref, right_ref,
    x_vmem, buffers, in_sems, out_sems,
):
    loads = [
        pltpu.make_async_copy(x_ref.at[pl.ds(k * BLK, BLK), :], x_vmem.at[k], in_sems.at[k]) for k in range(OWN)
    ]
    for load in loads:
        load.start()
    assign(pairs_ref, place_ref[0], place_ref[1], first_ref, second_ref, slot_ref, left_ref, right_ref)
    for k, load in enumerate(loads):
        load.wait()
        split_block(x_vmem[k], parts_ref, k, stats_ref, k)
    fill(0, EARLY_GROUPS, parts_ref, left_ref, right_ref, tiles_ref, buffers, out_sems)


def early(pairs, place, features):
    shots = features.shape[1]
    smem, vmem, anywhere = (pl.BlockSpec(memory_space=space) for space in (SMEM, VMEM, pl.ANY))
    numbers = jax.ShapeDtypeStruct((SLOTS,), jnp.int32)
    return pl.pallas_call(
        early_kernel,
        in_specs=[smem, smem, anywhere],
        out_specs=[anywhere, vmem, vmem] + [smem] * 5,
        out_shape=[
            pltpu.HBM((SHARDS, MADE, ROWS, BLK), F32),
            jax.ShapeDtypeStruct((PLACES * 2 * BLK, shots), BF16),
            jax.ShapeDtypeStruct((2, OWN, BLK), F32),
            numbers,
            numbers,
            jax.ShapeDtypeStruct((PAIRS,), jnp.int32),
            numbers,
            numbers,
        ],
        scratch_shapes=[
            VMEM((OWN, BLK, shots), F32),
            VMEM((EARLY, SHARDS, ROWS, BLK), F32),
            pltpu.SemaphoreType.DMA((OWN,)),
            pltpu.SemaphoreType.DMA((EARLY,)),
        ],
        compiler_params=pltpu.CompilerParams(vmem_limit_bytes=24 << 20),
        cost_estimate=pl.CostEstimate(flops=6 * EARLY * BLK * BLK * shots, bytes_accessed=12 << 20, transcendentals=0),
        name="early_tiles",
    )(pairs, place, pltpu.with_memory_space_constraint(features, pltpu.HBM))


def split_kernel(place, halo_ref, _, parts_ref):
    split_block(halo_ref[...], parts_ref, place, None, None)


def split(place, halo, parts):
    vmem = pl.BlockSpec(memory_space=VMEM)
    return pl.pallas_call(
        functools.partial(split_kernel, place),
        in_specs=[vmem, vmem],
        out_specs=vmem,
        out_shape=jax.ShapeDtypeStruct(parts.shape, BF16),
        input_output_aliases={1: 0},
        compiler_params=pltpu.CompilerParams(vmem_limit_bytes=8 << 20),
        cost_estimate=pl.CostEstimate(flops=SPLIT_COST, bytes_accessed=1 << 20, transcendentals=0),
        name="split_a",
    )(halo, parts)


def near_kernel(left_ref, right_ref, halo_ref, before_ref, _, tiles_ref, parts_ref, buffers, sems):

    def copy(k):
        return pltpu.make_async_copy(buffers.at[k], tiles_ref.at[:, EARLY + k], sems.at[k])

    with_b = MADE - EARLY - 3
    ahead = [product(before_ref, left_ref[EARLY + k], right_ref[EARLY + k]) for k in range(with_b, MADE - EARLY)]
    for k, tile in enumerate(ahead):
        buffers[with_b + k] = tile.reshape(SHARDS, ROWS, BLK)
        copy(with_b + k).start()
    for k in range(2):
        split_block(halo_ref[k * BLK : (k + 1) * BLK, :], parts_ref, OWN + k, None, None)
    fill(EARLY, (with_b,), parts_ref, left_ref, right_ref, tiles_ref, buffers, sems)
    for k in range(with_b, MADE - EARLY):
        copy(k).wait()


def near(left, right, halo, parts, tiles):
    smem, vmem, anywhere = (pl.BlockSpec(memory_space=space) for space in (SMEM, VMEM, pl.ANY))
    count = MADE - EARLY
    return pl.pallas_call(
        near_kernel,
        in_specs=[smem, smem, vmem, vmem, anywhere],
        out_specs=[anywhere, vmem],
        out_shape=[pltpu.HBM(tiles.shape, F32), jax.ShapeDtypeStruct(parts.shape, BF16)],
        scratch_shapes=[VMEM((count, SHARDS, ROWS, BLK), F32), pltpu.SemaphoreType.DMA((count,))],
        input_output_aliases={3: 1, 4: 0},
        compiler_params=pltpu.CompilerParams(vmem_limit_bytes=16 << 20),
        cost_estimate=pl.CostEstimate(
            flops=6 * count * BLK * BLK * halo.shape[1], bytes_accessed=5 << 20, transcendentals=0
        ),
        name="near_tiles",
    )(left, right, halo, parts, tiles)


def factors_kernel(
    count, first_ref, second_ref, me_ref, own_ref, below_ref, above_ref, main_ref, done_ref, shift_ref, scale_ref,
    turned, dev, inv, tiles, sem,
):
    fetch = pltpu.make_async_copy(main_ref, tiles, sem)
    fetch.start()
    shards = own_ref.shape[0]
    total = shards * count
    stats = jnp.concatenate([below_ref[...], own_ref[...], above_ref[...]], axis=2)
    means, squares = stats[:, 0], stats[:, 1]
    mean = jnp.sum(means, axis=0) * (1.0 / shards)
    away = means - mean[None]
    squares = jnp.sum(squares, axis=0) + count * jnp.sum(away * away, axis=0)
    inverse = lax.rsqrt(squares * (1.0 / total) + 1e-06)
    inv[...] = inverse
    for block in range(8):
        dev[block] = away[:, block, :]
    for block in range(OWN):
        column = jnp.concatenate(
            [away[:, 2 + block, :], jnp.broadcast_to(inverse[2 + block : 3 + block, :], (128 - shards, BLK))], axis=0
        )
        turned[block] = jnp.transpose(column)
    mine = pl.ds(pl.multiple_of(me_ref[0] * ROWS, ROWS), ROWS)
    for slot in range(SLOTS):
        a = jnp.clip(first_ref[slot], 0, OWN - 1)
        b = second_ref[slot] + 2
        left = turned[a, mine, :]
        shift = count * jnp.dot(
            left[:, :shards], dev[b], precision=lax.Precision.HIGHEST, preferred_element_type=F32
        )
        scale = left[:, shards : shards + 1] * inv[pl.ds(b, 1), :] * (1.0 / total**0.5)
        if slot == 0:
            fetch.wait()
        if slot == HOME:
            shift_ref[...] = shift
            scale_ref[...] = scale
        else:
            done_ref[slot] = (tiles[slot] + shift) * scale


def factors(count, first, second, me, own, below, above, main):
    vmem = pl.BlockSpec(memory_space=VMEM)
    smem = pl.BlockSpec(memory_space=SMEM)
    return pl.pallas_call(
        functools.partial(factors_kernel, count),
        in_specs=[smem] * 3 + [vmem] * 3 + [pl.BlockSpec(memory_space=pl.ANY)],
        out_specs=[vmem] * 3,
        out_shape=[jax.ShapeDtypeStruct((MADE, ROWS, BLK), F32)] + [jax.ShapeDtypeStruct((ROWS, BLK), F32)] * 2,
        scratch_shapes=[
            VMEM((OWN, BLK, 128), F32),
            VMEM((8, SHARDS, BLK), F32),
            VMEM((8, BLK), F32),
            VMEM((MADE, ROWS, BLK), F32),
            pltpu.SemaphoreType.DMA,
        ],
        compiler_params=pltpu.CompilerParams(vmem_limit_bytes=8 << 20),
        cost_estimate=pl.CostEstimate(flops=1 << 26, bytes_accessed=2 << 20, transcendentals=2048),
        name="factors",
    )(first, second, me, own, below, above, pltpu.with_memory_space_constraint(main, pltpu.HBM))


def finish_kernel(slot_ref, done_ref, home_ref, shift_ref, scale_ref, out_ref, home):
    home[...] = (home_ref[...] + shift_ref[...]) * scale_ref[...]
    for p in range(PAIRS):
        slot = slot_ref[p]
        made = done_ref[jnp.minimum(slot, MADE - 1)]
        out_ref[:, p, :] = jnp.where(slot == HOME, home[...], made)


def finish(slot, done, home, shift, scale):
    vmem = pl.BlockSpec(memory_space=VMEM)
    return pl.pallas_call(
        finish_kernel,
        in_specs=[pl.BlockSpec(memory_space=SMEM)] + [vmem] * 4,
        out_specs=vmem,
        out_shape=jax.ShapeDtypeStruct((ROWS, PAIRS, BLK), F32),
        scratch_shapes=[VMEM((ROWS, BLK), F32)],
        compiler_params=pltpu.CompilerParams(vmem_limit_bytes=8 << 20),
        cost_estimate=pl.CostEstimate(flops=1 << 18, bytes_accessed=1 << 20, transcendentals=0),
        name="finish",
    )(slot, done, home, shift, scale)


def on_device(features, pairs):
    shots = features.shape[1]
    owners = lax.axis_size("det")
    owner = lax.axis_index("det").astype(jnp.int32)
    core = lax.rem(owner, 2)
    place = jnp.stack([owner * OWN, core])
    me = lax.axis_index("shot").astype(jnp.int32).reshape(1)

    def swap(x, start):
        ends = [(i, i + 1) for i in range(start, owners - 1, 2)]
        return lax.ppermute(x, "det", ends + [(b, a) for a, b in ends])

    to_a = border(3 * core, 1, features, "border_for_a")
    later, to_a = lax.optimization_barrier((2 - 2 * core, to_a))
    from_a = swap(to_a, 1)
    from_b = swap(border(later, 2, features, "border_for_b"), 0)
    tiles, parts, stats, first, second, slot, left, right = early(pairs, place, features)
    parts = split(6, from_a, parts)
    tiles, _ = near(left, right, from_b, parts, tiles)
    main = lax.psum_scatter(
        tiles.reshape(SHARDS * MADE * ROWS, BLK), "shot", scatter_dimension=0, tiled=True
    ).reshape(MADE, ROWS, BLK)

    stats, tiles = lax.optimization_barrier((stats, tiles))
    stats = lax.all_gather(stats.reshape(2 * OWN, BLK), "shot").reshape(-1, 2, OWN, BLK)
    up = [(i, i + 1) for i in range(owners - 1)]
    below = lax.ppermute(stats[:, :, 2:], "det", up)
    above = lax.ppermute(stats[:, :, :2], "det", [(b, a) for a, b in up])
    home = swap(main[15], 1)
    done, shift, scale = factors(float(shots), first, second, me, stats, below, above, main)
    return finish(slot, done, home, shift, scale)


def solution(mesh):
    in_specs = (P("det", "shot"), P("det", None))
    out_specs = P("shot", "det", None)
    return jax.shard_map(on_device, mesh=mesh, in_specs=in_specs, out_specs=out_specs, check_vma=False)
```
